256 devices in a mesh: gz: 8 (over y, core), xy: 32 (over z, x).
Axes of the slice: x: 4, y: 4, z: 8, core: 2. Of those that a mesh axis runs over, the one named last changes fastest.
Arguments:
- velocity: float32 [8192, 8, 8, 128], P(('gz', 'xy')), may hold values from -6 to 6
- offset: int32 [8192], P(('gz', 'xy')), may hold values from 0 to 3
- interp_weight: float32 [8192], P(('gz', 'xy')), may hold values from 0.5 to 2
- route: int32 [8192, 1], replicated, may hold values from 0 to 31; in each aligned block of 32 rows (0 to 31, 32 to 63, ...) at most 4 rows name the same one
- dest_slot: int32 [8192], replicated, may hold values from 0 to 15
- conductivity: float32 [128, 2048, 128], P('gz', 'xy'), may hold values from -20 to 20
Outputs:
- update: bfloat16 [128, 2048, 128], P(None, 'xy')
The draws below stay inside these ranges and needn't reach their ends.
Inputs may be any that keep to these rules, and one draw needn't show every extreme that they name: `route`: in the records of one device (aligned blocks of 32 rows), no xy index is named more than 4 times, a bound that some block reaches.
All inputs are finite; a program needn't handle non-finite values.
Results may differ from the reference program's by a relative error of at most 0.0039.
Values may be sent and summed in bfloat16 or wider, within the bound.
No kernel may reach another device: no remote copies, remote signals or barrier semaphores. Data moves between devices by JAX's collectives and lax.ppermute only.
A program may use at most 64 MiB of HBM per device.

```python
import math
import jax
import jax.numpy as jnp
import numpy as np
from jax import lax

CX = 128
CZ = 16
CY = 64
SRC_DEV = 32
BZ = 8
BY = 8
CAP = 4
DB = 16
RECS = 8192
NZ = 128
NY = 2048
N_GZ = 8
N_XY = 32


def draw_conductivity(key, part):
    key = jax.random.fold_in(key, 3)
    depth_pos = jnp.arange(NZ, dtype=jnp.float32) / NZ
    lateral_pos = jnp.arange(NY, dtype=jnp.float32) / NY
    rough = jax.random.truncated_normal(key, -2.2, 2.2, (NZ, NY, CX), jnp.float32)
    amplitude = jnp.exp(math.log(3.0) * depth_pos)[:, None, None] * jnp.exp(math.log(3.0) * lateral_pos)[None, :, None]
    return rough * amplitude


def place_ends(drawn, own_key, low, largest):
    longest = drawn.shape.index(max(drawn.shape))
    spots = []
    for shift in (0, 1):
        where = [jax.random.randint(jax.random.fold_in(own_key, axis), (), 0, length) for axis, length in enumerate(drawn.shape)]
        where[longest] = (where[longest] + shift) % drawn.shape[longest]
        spots.append(tuple(where))
    return drawn.at[spots[0]].set(low).at[spots[1]].set(largest)


def steps_of(rng, dims, cuts, low, top_value):
    def one(dim, shards_of):
        draws = jax.random.uniform(jax.random.fold_in(jax.random.fold_in(rng, 6), dim), (shards_of,), jnp.float32, low / len(cuts), top_value / len(cuts))
        return jnp.repeat(jnp.exp(draws), dims[dim] // shards_of).reshape((-1,) + (1,) * (len(dims) - dim - 1))

    loudness = one(*cuts[0])
    for cut in cuts[1:]:
        loudness = loudness * one(*cut)
    return loudness


def assign_block(own_key, own, number, rows, number_of, top, bound, skew):
    order = jax.random.permutation(own_key, number_of)
    crowded, ordinary = portions_of(number_of, rows * top, bound, skew, True), portions_of(number_of, rows * top, bound, skew, False)
    places = jnp.arange(number_of)

    def named(tallies, turn):
        used = int((tallies > 0).sum())
        fixed = max(1, used // 4)
        passed = fixed + (places - fixed + turn * (used - fixed)) % max(1, number_of - fixed)
        return jnp.zeros((number_of,), jnp.int32).at[order[jnp.where(places < fixed, places, passed)]].set(jnp.asarray(tallies, jnp.int32))

    tallies = jnp.where(number % 4 == 0, named(crowded, number // 4), named(ordinary, number - number // 4 - 1))
    mixed = jax.random.permutation(jax.random.fold_in(own, 3), number_of)
    giver, sink = mixed[0:number_of // 2 * 2:2], mixed[1:number_of // 2 * 2:2]
    slack = jnp.minimum(tallies[giver] - 1, bound - tallies[sink]) // 2
    slack = jnp.where((giver == order[0]) | (sink == order[0]) | (tallies[sink] == 0), 0, jnp.maximum(slack, 0))
    passed = jax.random.randint(jax.random.fold_in(own, 4), (number_of // 2,), 0, 1 << 20) % (slack + 1)
    tallies = tallies.at[giver].add(-passed).at[sink].add(passed)
    labels = jnp.searchsorted(jnp.cumsum(tallies), jnp.arange(rows * top), side="right").astype(jnp.int32)
    table = labels.reshape(top, rows).T
    table = table[jax.random.permutation(jax.random.fold_in(own, 1), rows)]
    turn = jax.random.randint(jax.random.fold_in(own, 2), (rows, 1), 0, top)
    return jnp.take_along_axis(table, (jnp.arange(top)[None, :] + turn) % top, axis=1)


def portions_of(number_of, total, most, skew, full):
    portions = [(1 << 20) // math.isqrt(rank ** skew) + 1 for rank in range(1, number_of + 1)]
    largest = most if full else min(most, max(-(-total // number_of), total * portions[0] // sum(portions)))
    least = 1 if total - largest >= number_of - 1 else 0
    counts, spare = [largest] + [least] * (number_of - 1), total - largest - least * (number_of - 1)
    while spare > 0:
        movable = [i for i in range(1, number_of) if counts[i] < largest] or [i for i in range(1, number_of) if counts[i] < most]
        mass, remaining = sum([portions[i] for i in movable]), spare
        for i in movable:
            more = min(most - counts[i], max(1, remaining * portions[i] // mass), spare)
            counts[i] = counts[i] + more
            spare = spare - more
    return np.array(counts)


def centred(rng, shape, deviation, reach, shards=(), kind=jnp.bfloat16):
    array = deviation * jax.random.normal(rng, shape, jnp.float32)
    if shards:
        array = array * steps_of(rng, shape, shards, -0.22, 0.18)
    return jnp.clip(array, -reach, reach).astype(kind)


def setup_inputs(seed: int = 0) -> dict:
    key_list = jax.random.split(jax.random.key(seed), 7)
    velocity = centred(key_list[0], (RECS, BZ, BY, CX), 1.0, 6.0, ((0, 256),), jnp.float32)
    offset = place_ends(jax.random.randint(key_list[1], (RECS,), 0, 4), jax.random.fold_in(key_list[1], 1), 0, 3).astype(jnp.int32)
    interp_weight = jnp.clip(jnp.exp(math.log(2.0) - 1.3862944 * jax.random.uniform(key_list[2], (RECS,), jnp.float32) ** steps_of(key_list[2], (RECS,), ((0, 256),), -0.2, 0.2)), 0.5, 2.0)
    route_keys = jax.random.split(jax.random.fold_in(key_list[3], 1), RECS // SRC_DEV)
    route_turns = jax.random.permutation(jax.random.fold_in(key_list[3], 3), RECS // SRC_DEV)
    route = jax.vmap(lambda own, number: assign_block(jax.random.fold_in(key_list[3], 2), own, number, SRC_DEV, N_XY, 1, CAP, 2))(route_keys, route_turns).reshape((RECS, 1))
    dest_slot = place_ends(jax.random.randint(key_list[4], (RECS,), 0, DB), jax.random.fold_in(key_list[4], 1), 0, DB - 1).astype(jnp.int32)
    conductivity = draw_conductivity(jax.random.fold_in(key_list[6], 71), 0)
    return dict(velocity=velocity, offset=offset, interp_weight=interp_weight, route=route, dest_slot=dest_slot, conductivity=conductivity)


smooth_taps = (1.0 / 16.0, 4.0 / 16.0, 6.0 / 16.0, 4.0 / 16.0, 1.0 / 16.0)
deriv_taps = (1.0 / 12.0, -8.0 / 12.0, 0.0, 8.0 / 12.0, -1.0 / 12.0)

def taps_last(field, kernel):
    width = field.shape[-1]
    padded = jnp.pad(field, [(0, 0)] * (field.ndim - 1) + [(2, 2)])
    total = kernel[0] * padded[..., 0:width]
    for place in range(1, 5):
        if kernel[place] != 0.0:
            total = total + kernel[place] * padded[..., place:place + width]
    return total

def taps_along(field, kernel, axis):
    length = field.shape[axis] - 4
    total = kernel[0] * lax.slice_in_dim(field, 0, length, axis=axis)
    for place in range(1, 5):
        if kernel[place] != 0.0:
            total = total + kernel[place] * lax.slice_in_dim(field, place, place + length, axis=axis)
    return total

def grads(padded):
    axis_y = padded.ndim - 2
    axis_z = padded.ndim - 3
    smooth_x = taps_last(padded, smooth_taps)
    deriv_x = taps_last(padded, deriv_taps)
    grad_x = taps_along(taps_along(deriv_x, smooth_taps, axis_y), smooth_taps, axis_z)
    grad_y = taps_along(taps_along(smooth_x, deriv_taps, axis_y), smooth_taps, axis_z)
    grad_z = taps_along(taps_along(smooth_x, smooth_taps, axis_y), deriv_taps, axis_z)
    return (grad_x, grad_y, grad_z)

def cross_adjoint(grad_x, grad_y, grad_z):
    model_x, model_y, model_z = (grad_x[0], grad_y[0], grad_z[0])
    speed_x, speed_y, speed_z = (grad_x[1], grad_y[1], grad_z[1])
    cross_x = model_y * speed_z - model_z * speed_y
    cross_y = model_z * speed_x - model_x * speed_z
    cross_z = model_x * speed_y - model_y * speed_x
    adj_x = speed_y * cross_z - speed_z * cross_y
    adj_y = speed_z * cross_x - speed_x * cross_z
    adj_z = speed_x * cross_y - speed_y * cross_x
    return jnp.stack([adj_x, adj_y, adj_z])

def adjoint(padded):
    smooth_x = taps_last(padded[1:3], smooth_taps)
    deriv_x = taps_last(padded[0], deriv_taps)
    part_z = taps_along(smooth_x[1], smooth_taps, 1)
    part_rest = taps_along(smooth_x[0], deriv_taps, 1) + taps_along(deriv_x, smooth_taps, 1)
    return taps_along(part_z, deriv_taps, 0) + taps_along(part_rest, smooth_taps, 0)

def shifted_contrib(velocity, offset, interp_weight):
    width = velocity.shape[-1]
    padded = jnp.pad(velocity, ((0, 0), (0, 0), (0, 0), (0, 3)))
    moved = jnp.zeros_like(velocity)
    for step in range(4):
        moved = moved + jnp.where((offset == step)[:, None, None, None], padded[..., step:step + width], 0.0)
    return (interp_weight[:, None, None, None] * moved).astype(jnp.bfloat16)

def reference(velocity, offset, interp_weight, route, dest_slot, conductivity):
    contrib = shifted_contrib(velocity, offset, interp_weight).reshape(RECS, BZ * BY * CX).astype(jnp.float32)
    slab_of = jnp.arange(RECS, dtype=jnp.int32) // (N_XY * SRC_DEV)
    target = (slab_of * N_XY + route[:, 0]) * DB + dest_slot
    summed = jax.ops.segment_sum(contrib, target, num_segments=N_GZ * N_XY * DB)
    vgrid = summed.reshape(N_GZ, N_XY, CZ // BZ, CY // BY, BZ, BY, CX)
    vgrid = vgrid.transpose(0, 2, 4, 1, 3, 5, 6).reshape(NZ, NY, CX)
    fields = jnp.stack([conductivity, vgrid])
    padded = jnp.pad(fields, ((0, 0), (2, 2), (2, 2), (0, 0)))
    adj = cross_adjoint(*grads(padded))
    adj_pad = jnp.pad(adj, ((0, 0), (2, 2), (2, 2), (0, 0)))
    gradient = -adjoint(adj_pad)
    scale = 1.0 / jnp.sqrt(jnp.sum(gradient * gradient) / (NZ * NY * CX) + 1e-06)
    return (-gradient * scale).astype(jnp.bfloat16)
```

```python
import functools

import jax
import jax.numpy as jnp
from jax import lax
from jax.experimental import pallas as pl
from jax.experimental.pallas import tpu as pltpu
from jax.sharding import PartitionSpec as P

F32 = jnp.float32
BF16 = jnp.bfloat16
VMEM_LIMIT = 40 * 1024 * 1024
CAP = 4


def params():
    return pltpu.CompilerParams(vmem_limit_bytes=VMEM_LIMIT)


def vspec():
    return pl.BlockSpec(memory_space=pltpu.VMEM)


def sspec():
    return pl.BlockSpec(memory_space=pltpu.SMEM)


def sds(shape, dtype):
    return jax.ShapeDtypeStruct(shape, dtype)


def pack_kernel(vel, off, wt, route_any, route, slot, send, code, route_s, count, sem):
    g = lax.axis_index("gz")
    d = lax.axis_index("xy")
    rows = pl.ds(pl.multiple_of(g * 8, 8), 8)
    copy = pltpu.make_async_copy(route_any.at[rows], route_s, sem)
    copy.start()
    lane = lax.broadcasted_iota(jnp.int32, (8, 128), 1) % 32
    mine = (route[rows, :] == d).astype(jnp.int32)
    upto = mine
    for step in (1, 2, 4, 8, 16):
        upto = upto + jnp.where(lane >= step, pltpu.roll(upto, step, 1), 0)
    rank = upto - mine
    word = jnp.where(mine > 0, (slot[rows, :] + 1) << (5 * rank), 0)
    for step in (1, 2, 4, 8, 16):
        word = word + jnp.where(lane >= step, pltpu.roll(word, step, 1), 0)
    code[...] = word
    for i in range(32):
        count[i] = 0
    copy.wait()
    row = d // 4
    first = (d % 4) * 32
    x = lax.broadcasted_iota(jnp.int32, (64, 128), 1)

    def one(r, carry):
        dest = route_s[row, first + r]
        k = count[dest]
        count[dest] = k + 1
        o = off[r]
        v = vel[r].reshape(64, 128)
        moved = jnp.where(x < 128 - o, pltpu.roll(v, (128 - o) % 128, 1), 0.0)
        send[dest * CAP + k] = (moved * wt[r]).astype(BF16)
        return carry

    lax.fori_loop(0, 32, one, 0)


def pack(velocity, offset, weight, route, slot):
    return pl.pallas_call(
        pack_kernel,
        out_shape=(sds((32 * CAP, 64, 128), BF16), sds((8, 128), jnp.int32)),
        in_specs=[vspec(), sspec(), sspec(), pl.BlockSpec(memory_space=pl.ANY), vspec(), vspec()],
        out_specs=(vspec(), vspec()),
        scratch_shapes=[
            pltpu.SMEM((8, 128), jnp.int32),
            pltpu.SMEM((32,), jnp.int32),
            pltpu.SemaphoreType.DMA,
        ],
        compiler_params=params(),
        name="pack",
    )(velocity, offset, weight, route, route, slot)


def pair_rows(block):
    n = block.shape[0] // 2
    return jnp.stack(
        [jnp.concatenate([block[2 * i], block[2 * i + 1]], axis=0) for i in range(n)]
    )


def combine_kernel(recv, code, cond, v, z_a, z_b, y_own):
    g = lax.axis_index("gz")
    d = lax.axis_index("xy")
    v[...] = jnp.zeros_like(v)

    def source(s, carry):
        word = code[s // 4, (s % 4) * 32 + 31]
        for k in range(CAP):
            j = ((word >> (5 * k)) & 31) - 1

            @pl.when(j >= 0)
            def _():
                z0 = pl.multiple_of((j // 8) * 8, 8)
                y0 = pl.multiple_of((j % 8) * 8, 8)
                block = recv[s * CAP + k].astype(F32).reshape(8, 8, 128)
                v[pl.ds(z0, 8), pl.ds(y0, 8), :] += block

        return carry

    lax.fori_loop(0, 32, source, 0)
    even = g % 2 == 0
    z_hi = jnp.where(even, 12, 0)
    z_lo = 12 - z_hi
    y_even = d % 2 == 0
    for f, field in enumerate((cond, v)):
        z_a[f] = field[pl.ds(z_hi, 4)]
        z_b[f] = field[pl.ds(z_lo, 4)]
        lo = pair_rows(field[:, 0:8, :][:, 0:4])
        hi = pair_rows(field[:, 56:64, :][:, 4:8])
        y_own[0, f] = jnp.where(y_even, hi, lo)
        y_own[1, f] = jnp.where(y_even, lo, hi)


def combine(recv, code, cond):
    return pl.pallas_call(
        combine_kernel,
        out_shape=(
            sds((16, 64, 128), F32),
            sds((2, 4, 64, 128), F32),
            sds((2, 4, 64, 128), F32),
            sds((2, 2, 8, 8, 128), F32),
        ),
        in_specs=[vspec(), sspec(), vspec()],
        out_specs=(vspec(),) * 4,
        compiler_params=params(),
        name="combine",
    )(recv, code, cond)


def strips_kernel(y_own, r_a, r_b, y_c, y_d):
    d = lax.axis_index("xy")
    y_even = d % 2 == 0
    for f in range(2):
        y_c[f, 0:8] = y_own[0, f]
        y_d[f, 0:8] = y_own[1, f]
        for i, r in enumerate((r_a, r_b)):
            lo = pair_rows(r[f, :, 0:8, :][:, 0:4])
            hi = pair_rows(r[f, :, 56:64, :][:, 4:8])
            at = slice(8 + 2 * i, 10 + 2 * i)
            y_c[f, at] = jnp.where(y_even, hi, lo)
            y_d[f, at] = jnp.where(y_even, lo, hi)


def strips(y_own, r_a, r_b):
    return pl.pallas_call(
        strips_kernel,
        out_shape=(sds((2, 12, 8, 128), F32),) * 2,
        in_specs=[vspec()] * 3,
        out_specs=(vspec(),) * 2,
        compiler_params=params(),
        name="strips",
    )(y_own, r_a, r_b)


def split3(x):
    hi = x.astype(BF16)
    rest = x - hi.astype(F32)
    mid = rest.astype(BF16)
    lo = (rest - mid.astype(F32)).astype(BF16)
    return hi, mid, lo


def band(taps):
    i = lax.broadcasted_iota(jnp.int32, (128, 128), 0)
    j = lax.broadcasted_iota(jnp.int32, (128, 128), 1)
    m = jnp.zeros((128, 128), F32)
    for place, tap in enumerate(taps):
        if tap:
            m = jnp.where(i - j == place - 2, F32(tap), m)
    return m.astype(BF16)


S_TAPS = (1.0, 4.0, 6.0, 4.0, 1.0)
D_TAPS = (1.0, -8.0, 0.0, 8.0, -1.0)
NORM = 1.0 / (16.0 * 16.0 * 12.0)


def smooth5(a):
    return (a[0] + a[4]) + 4.0 * (a[1] + a[3]) + 6.0 * a[2]


def deriv5(a):
    return (a[0] - a[4]) + 8.0 * (a[3] - a[1])


def dot(a, b):
    return jnp.dot(a, b, preferred_element_type=F32)


def stencil_kernel(cond, v, r_a, r_b, q_c, q_d, out, total, ext, sx, dx, adj, mid_u, mid_t):
    g = lax.axis_index("gz")
    d = lax.axis_index("xy")
    even = g % 2 == 0
    y_even = d % 2 == 0
    at_a = jnp.where(even, 20, 0)
    at_b = 20 - at_a
    low_in = (g > 0).astype(F32)
    high_in = (g < 7).astype(F32)
    keep_a = jnp.where(even, high_in, low_in)
    keep_b = jnp.where(even, low_in, high_in)
    left_in = (d > 0).astype(F32)
    right_in = (d < 31).astype(F32)
    zeros4 = jnp.zeros((4, 128), F32)
    for f, field in enumerate((cond, v)):
        ext[f, 4:20, 8:72, :] = field[...]
        ext[f, pl.ds(at_a, 4), 8:72, :] = r_a[f] * keep_a
        ext[f, pl.ds(at_b, 4), 8:72, :] = r_b[f] * keep_b
        for z in range(24):
            c = q_c[f, z // 2]
            e = q_d[f, z // 2]
            lo = jnp.where(y_even, e, c)[4 * (z % 2) : 4 * (z % 2) + 4] * left_in
            hi = jnp.where(y_even, c, e)[4 * (z % 2) : 4 * (z % 2) + 4] * right_in
            if z < 16:
                place, keep = z + 4, 1.0
            elif z < 20:
                place, keep = at_a + (z - 16), keep_a
            else:
                place, keep = at_b + (z - 20), keep_b
            ext[f, place, 0:8, :] = jnp.concatenate([zeros4, lo * keep], axis=0)
            ext[f, place, 72:80, :] = jnp.concatenate([hi * keep, zeros4], axis=0)

    weights = jnp.concatenate([band(S_TAPS), band(D_TAPS)], axis=1)

    def along_x(i, carry):
        f = i // 24
        z = i % 24
        h, m, l = split3(ext[f, z])
        both = dot(h, weights) + dot(m, weights) + dot(l, weights)
        sx[f, z] = both[:, 0:128]
        dx[f, z] = both[:, 128:256]
        return carry

    lax.fori_loop(0, 48, along_x, 0)

    def along_y(i, carry):
        f = i // 24
        z = i % 24
        s = sx[f, z]
        t = dx[f, z]
        ss = [pltpu.roll(s, sh % 80, 0) for sh in (2, 1, 0, -1, -2)]
        tt = [pltpu.roll(t, sh % 80, 0) for sh in (2, 1, 0, -1, -2)]
        dx[f, z] = smooth5(tt)
        sx[f, z] = deriv5(ss)
        ext[f, z] = smooth5(ss)
        return carry

    lax.fori_loop(0, 48, along_y, 0)

    row = lax.broadcasted_iota(jnp.int32, (8, 128), 0)

    def cross(t, carry):
        y0 = pl.multiple_of(t * 8, 8)
        y = row + (y0 - 8)
        inside = jnp.where((y >= 0) | (d > 0), NORM, 0.0)
        inside = jnp.where((y < 64) | (d < 31), inside, 0.0)
        tile = pl.ds(y0, 8)
        for z in range(20):
            scale = inside
            if z < 2:
                scale = inside * low_in
            if z >= 18:
                scale = inside * high_in
            grad = []
            for f in range(2):
                gx = smooth5([dx[f, z + i, tile, :] for i in range(5)]) * scale
                gy = smooth5([sx[f, z + i, tile, :] for i in range(5)]) * scale
                gz = deriv5([ext[f, z + i, tile, :] for i in range(5)]) * scale
                grad.append((gx, gy, gz))
            (mx, my, mz), (vx, vy, vz) = grad
            cx = my * vz - mz * vy
            cy = mz * vx - mx * vz
            cz = mx * vy - my * vx
            adj[0, z, tile, :] = vy * cz - vz * cy
            adj[1, z, tile, :] = vz * cx - vx * cz
            adj[2, z, tile, :] = vx * cy - vy * cx
        return carry

    lax.fori_loop(0, 10, cross, 0)

    def back_yz(z, carry):
        p = smooth5([adj[0, z + i] for i in range(5)])
        q = smooth5([adj[1, z + i] for i in range(5)])
        r = deriv5([adj[2, z + i] for i in range(5)])
        sh = lambda a: [pltpu.roll(a, s % 80, 0) for s in (2, 1, 0, -1, -2)]
        mid_u[z] = smooth5(sh(p))[8:72]
        mid_t[z] = (deriv5(sh(q)) + smooth5(sh(r)))[8:72]
        return carry

    lax.fori_loop(0, 16, back_yz, 0)

    w_s = band(S_TAPS)
    w_d = band(D_TAPS)
    w = jnp.concatenate([w_d, w_s], axis=0)
    total[...] = jnp.zeros_like(total)

    def back_x(z, carry):
        us = split3(mid_u[z])
        ts = split3(mid_t[z])
        acc = sum(dot(jnp.concatenate([a, b], axis=1), w) for a, b in zip(us, ts))
        acc = acc * NORM
        out[z] = acc.astype(BF16)
        total[...] += jnp.sum((acc * acc).reshape(8, 8, 128), axis=0)
        return carry

    lax.fori_loop(0, 16, back_x, 0)
    total[...] = jnp.broadcast_to(jnp.sum(total[...], axis=0, keepdims=True), (8, 128))


def stencil(cond, v, r_a, r_b, q_c, q_d):
    return pl.pallas_call(
        stencil_kernel,
        out_shape=(sds((16, 64, 128), BF16), sds((8, 128), F32)),
        in_specs=[vspec()] * 6,
        out_specs=(vspec(),) * 2,
        scratch_shapes=[
            pltpu.VMEM((2, 24, 80, 128), F32),
            pltpu.VMEM((2, 24, 80, 128), F32),
            pltpu.VMEM((2, 24, 80, 128), F32),
            pltpu.VMEM((3, 20, 80, 128), F32),
            pltpu.VMEM((16, 64, 128), F32),
            pltpu.VMEM((16, 64, 128), F32),
        ],
        compiler_params=params(),
        name="stencil",
    )(cond, v, r_a, r_b, q_c, q_d)


def scale_kernel(cells, sums, *refs):
    pieces, out = refs[:-1], refs[-1]
    g = lax.axis_index("gz")
    total = jnp.sum(sums[...], axis=0, keepdims=True)
    total = jnp.sum(total, axis=1, keepdims=True)
    scale = 1.0 / jnp.sqrt(total / cells + 1e-06)
    scale = jnp.broadcast_to(scale, (64, 128))
    for k, piece in enumerate(pieces):
        base = (g ^ k) * 16
        for z in range(16):
            out[base + z] = (piece[z].astype(F32) * scale).astype(BF16)


def scaled(cells, sums, pieces):
    return pl.pallas_call(
        functools.partial(scale_kernel, cells),
        out_shape=sds((128, 64, 128), BF16),
        in_specs=[vspec()] * (1 + len(pieces)),
        out_specs=vspec(),
        compiler_params=params(),
        name="scale",
    )(sums, *pieces)


def swap_odd(count):
    return [(i, (i + 1) % count if i % 2 else (i - 1) % count) for i in range(count)]


def swap_even(count):
    return [(i, i ^ 1) for i in range(count)]


def local(velocity, offset, interp_weight, route, dest_slot, conductivity):
    n_g = lax.axis_size("gz")
    n_x = lax.axis_size("xy")
    send, code = pack(
        velocity, offset, interp_weight, route.reshape(64, 128), dest_slot.reshape(64, 128)
    )
    recv = lax.all_to_all(
        send.reshape(n_x, CAP * 64, 128), "xy", split_axis=0, concat_axis=0, tiled=True
    )
    v, z_a, z_b, y_own = combine(recv.reshape(n_x * CAP, 64, 128), code, conductivity)
    r_a = lax.ppermute(z_a, "gz", swap_even(n_g))
    r_b = lax.ppermute(z_b, "gz", swap_odd(n_g))
    y_c, y_d = strips(y_own, r_a, r_b)
    q_c = lax.ppermute(y_c, "xy", swap_even(n_x))
    q_d = lax.ppermute(y_d, "xy", swap_odd(n_x))
    grad, total = stencil(conductivity, v, r_a, r_b, q_c, q_d)
    pieces = [grad]
    for k in range(1, n_g):
        pieces.append(lax.ppermute(grad, "gz", [(i, i ^ k) for i in range(n_g)]))
    part = jnp.broadcast_to(total[0:1], (n_x, 128))
    part = lax.all_to_all(part, "xy", 0, 0, tiled=True)
    part = jnp.broadcast_to(jnp.sum(part, axis=0, keepdims=True), (n_g, 128))
    part = lax.all_to_all(part, "gz", 0, 0, tiled=True)
    cells = float(n_g * n_x * 16 * 64 * 128)
    return scaled(cells, part, pieces)


def solution(mesh):
    in_specs = (
        P(("gz", "xy"), None, None, None),
        P(("gz", "xy")),
        P(("gz", "xy")),
        P(),
        P(),
        P("gz", "xy", None),
    )
    out_specs = P(None, "xy", None)
    return jax.shard_map(local, mesh=mesh, in_specs=in_specs, out_specs=out_specs, check_vma=False)
```

```python
import functools

import jax
import jax.numpy as jnp
from jax import lax
from jax.experimental import pallas as pl
from jax.experimental.pallas import tpu as pltpu
from jax.sharding import PartitionSpec as P

F32 = jnp.float32
BF16 = jnp.bfloat16
VMEM_LIMIT = 24 * 1024 * 1024
VMEM_ALL = 60 * 1024 * 1024
CAP = 4


def params(limit=VMEM_LIMIT):
    return pltpu.CompilerParams(vmem_limit_bytes=limit)


def vspec():
    return pl.BlockSpec(memory_space=pltpu.VMEM)


def sspec():
    return pl.BlockSpec(memory_space=pltpu.SMEM)


def sds(shape, dtype):
    return jax.ShapeDtypeStruct(shape, dtype)


def pack_kernel(vel_any, off, wt, route_any, slot_any, send, code, vel, out, route, slot, route_s, count, sems):
    g = lax.axis_index("gz")
    d = lax.axis_index("xy")
    rows = pl.ds(pl.multiple_of(g * 8, 8), 8)
    loads = [
        pltpu.make_async_copy(route_any.at[rows], route_s, sems.at[0]),
        pltpu.make_async_copy(route_any.at[rows], route, sems.at[1]),
        pltpu.make_async_copy(slot_any.at[rows], slot, sems.at[2]),
    ]
    bricks = [
        pltpu.make_async_copy(vel_any.at[pl.ds(8 * i, 8)], vel.at[pl.ds(8 * i, 8)], sems.at[3 + i])
        for i in range(4)
    ]
    for copy in loads + bricks:
        copy.start()
    for i in range(32):
        count[i] = 0
    for copy in loads:
        copy.wait()
    lane = lax.broadcasted_iota(jnp.int32, (8, 128), 1) % 32
    mine = (route[...] == d).astype(jnp.int32)
    upto = mine
    for step in (1, 2, 4, 8, 16):
        upto = upto + jnp.where(lane >= step, pltpu.roll(upto, step, 1), 0)
    rank = upto - mine
    word = jnp.where(mine > 0, (slot[...] + 1) << (5 * rank), 0)
    for step in (1, 2, 4, 8, 16):
        word = word + jnp.where(lane >= step, pltpu.roll(word, step, 1), 0)
    code[...] = word
    row = d // 4
    first = (d % 4) * 32
    x = lax.broadcasted_iota(jnp.int32, (64, 128), 1)
    for r in range(32):
        if r % 8 == 0:
            bricks[r // 8].wait()
        dest = route_s[row, first + r]
        k = count[dest]
        count[dest] = k + 1
        o = off[r]
        v = vel[r].reshape(64, 128)
        moved = jnp.where(x < 128 - o, pltpu.roll(v, (128 - o) % 128, 1), 0.0)
        out[r] = (moved * wt[r]).astype(BF16)
        pltpu.make_async_copy(out.at[r], send.at[dest * CAP + k], sems.at[7]).start()
    pltpu.make_async_copy(out, send.at[pl.ds(0, 32)], sems.at[7]).wait()


def pack(velocity, offset, weight, route, slot):
    anywhere = pl.BlockSpec(memory_space=pl.ANY)
    return pl.pallas_call(
        pack_kernel,
        out_shape=(sds((32 * CAP, 64, 128), BF16), sds((8, 128), jnp.int32)),
        in_specs=[anywhere, sspec(), sspec(), anywhere, anywhere],
        out_specs=(anywhere, vspec()),
        scratch_shapes=[
            pltpu.VMEM((32, 8, 8, 128), F32),
            pltpu.VMEM((32, 64, 128), BF16),
            pltpu.VMEM((8, 128), jnp.int32),
            pltpu.VMEM((8, 128), jnp.int32),
            pltpu.SMEM((8, 128), jnp.int32),
            pltpu.SMEM((32,), jnp.int32),
            pltpu.SemaphoreType.DMA((8,)),
        ],
        compiler_params=params(VMEM_ALL),
        name="pack",
    )(velocity, offset, weight, route, slot)


def pair_rows(block):
    n = block.shape[0] // 2
    return jnp.stack(
        [jnp.concatenate([block[2 * i], block[2 * i + 1]], axis=0) for i in range(n)]
    )


def combine_kernel(recv, code, cond, v, z_a, z_b, y_own):
    g = lax.axis_index("gz")
    d = lax.axis_index("xy")
    v[...] = jnp.zeros_like(v)

    def source(s, carry):
        word = code[s // 4, (s % 4) * 32 + 31]
        for k in range(CAP):
            j = ((word >> (5 * k)) & 31) - 1

            @pl.when(j >= 0)
            def _():
                z0 = pl.multiple_of((j // 8) * 8, 8)
                y0 = pl.multiple_of((j % 8) * 8, 8)
                block = recv[s * CAP + k].astype(F32).reshape(8, 8, 128)
                v[pl.ds(z0, 8), pl.ds(y0, 8), :] += block

        return carry

    lax.fori_loop(0, 32, source, 0)
    even = g % 2 == 0
    z_hi = jnp.where(even, 12, 0)
    z_lo = 12 - z_hi
    y_even = d % 2 == 0
    for f, field in enumerate((cond, v)):
        z_a[f] = field[pl.ds(z_hi, 4)]
        z_b[f] = field[pl.ds(z_lo, 4)]
        lo = pair_rows(field[:, 0:8, :][:, 0:4])
        hi = pair_rows(field[:, 56:64, :][:, 4:8])
        y_own[0, f] = jnp.where(y_even, hi, lo)
        y_own[1, f] = jnp.where(y_even, lo, hi)


def combine(recv, code, cond):
    return pl.pallas_call(
        combine_kernel,
        out_shape=(
            sds((16, 64, 128), F32),
            sds((2, 4, 64, 128), F32),
            sds((2, 4, 64, 128), F32),
            sds((2, 2, 8, 8, 128), F32),
        ),
        in_specs=[vspec(), sspec(), vspec()],
        out_specs=(vspec(),) * 4,
        compiler_params=params(),
        name="combine",
    )(recv, code, cond)


def strips_kernel(y_own, r_a, r_b, y_c, y_d):
    d = lax.axis_index("xy")
    y_even = d % 2 == 0
    for f in range(2):
        y_c[f, 0:8] = y_own[0, f]
        y_d[f, 0:8] = y_own[1, f]
        for i, r in enumerate((r_a, r_b)):
            lo = pair_rows(r[f, :, 0:8, :][:, 0:4])
            hi = pair_rows(r[f, :, 56:64, :][:, 4:8])
            at = slice(8 + 2 * i, 10 + 2 * i)
            y_c[f, at] = jnp.where(y_even, hi, lo)
            y_d[f, at] = jnp.where(y_even, lo, hi)


def strips(y_own, r_a, r_b):
    return pl.pallas_call(
        strips_kernel,
        out_shape=(sds((2, 12, 8, 128), F32),) * 2,
        in_specs=[vspec()] * 3,
        out_specs=(vspec(),) * 2,
        compiler_params=params(),
        name="strips",
    )(y_own, r_a, r_b)


def split3(x):
    hi = x.astype(BF16)
    rest = x - hi.astype(F32)
    mid = rest.astype(BF16)
    lo = (rest - mid.astype(F32)).astype(BF16)
    return hi, mid, lo


def band(taps):
    i = lax.broadcasted_iota(jnp.int32, (128, 128), 0)
    j = lax.broadcasted_iota(jnp.int32, (128, 128), 1)
    m = jnp.zeros((128, 128), F32)
    for place, tap in enumerate(taps):
        if tap:
            m = jnp.where(i - j == place - 2, F32(tap), m)
    return m.astype(BF16)


S_TAPS = (1.0, 4.0, 6.0, 4.0, 1.0)
D_TAPS = (1.0, -8.0, 0.0, 8.0, -1.0)
NORM = 1.0 / (16.0 * 16.0 * 12.0)


def smooth5(a):
    return (a[0] + a[4]) + 4.0 * (a[1] + a[3]) + 6.0 * a[2]


def deriv5(a):
    return (a[0] - a[4]) + 8.0 * (a[3] - a[1])


def dot(a, b):
    return jnp.dot(a, b, preferred_element_type=F32)


def stencil_kernel(cond, v, r_a, r_b, q_c, q_d, out, total, ext, sx, dx, adj, mid_u, mid_t):
    g = lax.axis_index("gz")
    d = lax.axis_index("xy")
    even = g % 2 == 0
    y_even = d % 2 == 0
    at_a = jnp.where(even, 20, 0)
    at_b = 20 - at_a
    low_in = (g > 0).astype(F32)
    high_in = (g < 7).astype(F32)
    keep_a = jnp.where(even, high_in, low_in)
    keep_b = jnp.where(even, low_in, high_in)
    left_in = (d > 0).astype(F32)
    right_in = (d < 31).astype(F32)
    zeros4 = jnp.zeros((4, 128), F32)
    for f, field in enumerate((cond, v)):
        ext[f, 4:20, 8:72, :] = field[...]
        ext[f, pl.ds(at_a, 4), 8:72, :] = r_a[f] * keep_a
        ext[f, pl.ds(at_b, 4), 8:72, :] = r_b[f] * keep_b
        for z in range(24):
            c = q_c[f, z // 2]
            e = q_d[f, z // 2]
            lo = jnp.where(y_even, e, c)[4 * (z % 2) : 4 * (z % 2) + 4] * left_in
            hi = jnp.where(y_even, c, e)[4 * (z % 2) : 4 * (z % 2) + 4] * right_in
            if z < 16:
                place, keep = z + 4, 1.0
            elif z < 20:
                place, keep = at_a + (z - 16), keep_a
            else:
                place, keep = at_b + (z - 20), keep_b
            ext[f, place, 0:8, :] = jnp.concatenate([zeros4, lo * keep], axis=0)
            ext[f, place, 72:80, :] = jnp.concatenate([hi * keep, zeros4], axis=0)

    weights = jnp.concatenate([band(S_TAPS), band(D_TAPS)], axis=1)

    twice = jnp.concatenate([weights, weights], axis=0)

    def along_x(i, carry):
        f = i // 2
        part = pl.ds((i % 2) * 12, 12)
        h, m, l = split3(ext[f, part].reshape(12 * 80, 128))
        both = dot(jnp.concatenate([h, m], axis=1), twice) + dot(l, weights)
        sx[f, part] = both[:, 0:128].reshape(12, 80, 128)
        dx[f, part] = both[:, 128:256].reshape(12, 80, 128)
        return carry

    lax.fori_loop(0, 4, along_x, 0)

    def along_y(i, carry):
        f = i // 24
        z = i % 24
        s = sx[f, z]
        t = dx[f, z]
        ss = [pltpu.roll(s, sh % 80, 0) for sh in (2, 1, 0, -1, -2)]
        tt = [pltpu.roll(t, sh % 80, 0) for sh in (2, 1, 0, -1, -2)]
        dx[f, z] = smooth5(tt)
        sx[f, z] = deriv5(ss)
        ext[f, z] = smooth5(ss)
        return carry

    lax.fori_loop(0, 48, along_y, 0, unroll=2)

    row = lax.broadcasted_iota(jnp.int32, (8, 128), 0)

    def cross(t, carry):
        y0 = pl.multiple_of(t * 8, 8)
        y = row + (y0 - 8)
        inside = jnp.where((y >= 0) | (d > 0), NORM, 0.0)
        inside = jnp.where((y < 64) | (d < 31), inside, 0.0)
        tile = pl.ds(y0, 8)
        for z in range(20):
            scale = inside
            if z < 2:
                scale = inside * low_in
            if z >= 18:
                scale = inside * high_in
            grad = []
            for f in range(2):
                gx = smooth5([dx[f, z + i, tile, :] for i in range(5)]) * scale
                gy = smooth5([sx[f, z + i, tile, :] for i in range(5)]) * scale
                gz = deriv5([ext[f, z + i, tile, :] for i in range(5)]) * scale
                grad.append((gx, gy, gz))
            (mx, my, mz), (vx, vy, vz) = grad
            cx = my * vz - mz * vy
            cy = mz * vx - mx * vz
            cz = mx * vy - my * vx
            adj[0, z, tile, :] = vy * cz - vz * cy
            adj[1, z, tile, :] = vz * cx - vx * cz
            adj[2, z, tile, :] = vx * cy - vy * cx
        return carry

    lax.fori_loop(0, 10, cross, 0)

    def back_yz(z, carry):
        p = smooth5([adj[0, z + i] for i in range(5)])
        q = smooth5([adj[1, z + i] for i in range(5)])
        r = deriv5([adj[2, z + i] for i in range(5)])
        sh = lambda a: [pltpu.roll(a, s % 80, 0) for s in (2, 1, 0, -1, -2)]
        mid_u[z] = smooth5(sh(p))[8:72]
        mid_t[z] = (deriv5(sh(q)) + smooth5(sh(r)))[8:72]
        return carry

    lax.fori_loop(0, 16, back_yz, 0)

    w_s = band(S_TAPS)
    w_d = band(D_TAPS)
    w = jnp.concatenate([w_d, w_s], axis=0)
    total[0:8, :] = jnp.zeros((8, 128), F32)

    def back_x(i, carry):
        part = pl.ds(i * 8, 8)
        us = split3(mid_u[part].reshape(512, 128))
        ts = split3(mid_t[part].reshape(512, 128))
        acc = sum(dot(jnp.concatenate([a, b], axis=1), w) for a, b in zip(us, ts))
        acc = acc * NORM
        out[part] = acc.reshape(8, 64, 128).astype(BF16)
        total[0:8, :] += jnp.sum((acc * acc).reshape(64, 8, 128), axis=0)
        return carry

    lax.fori_loop(0, 2, back_x, 0, unroll=2)
    total[...] = jnp.broadcast_to(jnp.sum(total[0:8, :], axis=0, keepdims=True), (32, 128))


def stencil(cond, v, r_a, r_b, q_c, q_d):
    return pl.pallas_call(
        stencil_kernel,
        out_shape=(sds((16, 64, 128), BF16), sds((32, 128), F32)),
        in_specs=[vspec()] * 6,
        out_specs=(vspec(),) * 2,
        scratch_shapes=[
            pltpu.VMEM((2, 24, 80, 128), F32),
            pltpu.VMEM((2, 24, 80, 128), F32),
            pltpu.VMEM((2, 24, 80, 128), F32),
            pltpu.VMEM((3, 20, 80, 128), F32),
            pltpu.VMEM((16, 64, 128), F32),
            pltpu.VMEM((16, 64, 128), F32),
        ],
        compiler_params=params(),
        name="stencil",
    )(cond, v, r_a, r_b, q_c, q_d)


def scale_kernel(cells, sums, pair, before, after, far_own, far_twin, out):
    g = lax.axis_index("gz")
    total = jnp.sum(sums[...], axis=0, keepdims=True)
    total = jnp.sum(total, axis=1, keepdims=True)
    scale = 1.0 / jnp.sqrt(total / cells + 1e-06)
    scale = jnp.broadcast_to(scale, (64, 128))
    left, right, across = lax.rem(g + 6, 8), lax.rem(g + 2, 8), lax.rem(g + 4, 8)
    places = [(pair.at[0], g), (pair.at[1], g ^ 1)]
    places += [(before.at[0], left), (before.at[1], left ^ 1)]
    places += [(after.at[0], right), (after.at[1], right ^ 1)]
    places += [(far_own, across), (far_twin, across ^ 1)]
    for piece, owner in places:
        for z in range(16):
            out[owner * 16 + z] = (piece[z].astype(F32) * scale).astype(BF16)


def scaled(cells, sums, pieces):
    return pl.pallas_call(
        functools.partial(scale_kernel, cells),
        out_shape=sds((128, 64, 128), BF16),
        in_specs=[vspec()] * (1 + len(pieces)),
        out_specs=vspec(),
        compiler_params=params(),
        name="scale",
    )(sums, *pieces)


def swap_odd(count):
    return [(i, (i + 1) % count if i % 2 else (i - 1) % count) for i in range(count)]


def swap_even(count):
    return [(i, i ^ 1) for i in range(count)]


def row_sum(rows, size):
    return jnp.broadcast_to(jnp.sum(rows, axis=0, keepdims=True), (size, 128))


def local(velocity, offset, interp_weight, route, dest_slot, conductivity):
    n_g = lax.axis_size("gz")
    n_x = lax.axis_size("xy")
    send, code = pack(
        velocity, offset, interp_weight, route.reshape(64, 128), dest_slot.reshape(64, 128)
    )
    recv = lax.all_to_all(
        send.reshape(n_x, CAP * 64, 128), "xy", split_axis=0, concat_axis=0, tiled=True
    )
    v, z_a, z_b, y_own = combine(recv.reshape(n_x * CAP, 64, 128), code, conductivity)
    r_a = lax.ppermute(z_a, "gz", swap_even(n_g))
    r_b = lax.ppermute(z_b, "gz", swap_odd(n_g))
    y_c, y_d = strips(y_own, r_a, r_b)
    q_c = lax.ppermute(y_c, "xy", swap_even(n_x))
    q_d = lax.ppermute(y_d, "xy", swap_odd(n_x))
    grad, total = stencil(conductivity, v, r_a, r_b, q_c, q_d)
    up = [(i, (i + 2) % n_g) for i in range(n_g)]
    down = [(i, (i - 2) % n_g) for i in range(n_g)]
    pair = jnp.stack([grad, lax.ppermute(grad, "gz", swap_even(n_g))])
    pair, total = lax.optimization_barrier((pair, total))
    before = lax.ppermute(pair, "gz", up)
    after = lax.ppermute(pair, "gz", down)
    rows = lax.all_to_all(total, "xy", 0, 0, tiled=True)
    before, after, rows = lax.optimization_barrier((before, after, rows))
    far_own = lax.ppermute(before[0], "gz", up)
    far_twin = lax.ppermute(after[1], "gz", down)
    sums = lax.all_to_all(row_sum(rows, n_g), "gz", 0, 0, tiled=True)
    pieces = [pair, before, after, far_own, far_twin]
    cells = float(n_g * n_x * 16 * 64 * 128)
    return scaled(cells, sums, pieces)


def solution(mesh):
    in_specs = (
        P(("gz", "xy"), None, None, None),
        P(("gz", "xy")),
        P(("gz", "xy")),
        P(),
        P(),
        P("gz", "xy", None),
    )
    out_specs = P(None, "xy", None)
    return jax.shard_map(local, mesh=mesh, in_specs=in_specs, out_specs=out_specs, check_vma=False)
```

```python
import functools

import jax
import jax.numpy as jnp
from jax import lax
from jax.experimental import pallas as pl
from jax.experimental.pallas import tpu as pltpu
from jax.sharding import PartitionSpec as P

F32 = jnp.float32
BF16 = jnp.bfloat16
VMEM_LIMIT = 24 * 1024 * 1024
VMEM_ALL = 60 * 1024 * 1024
CAP = 4


def params(limit=VMEM_LIMIT):
    return pltpu.CompilerParams(vmem_limit_bytes=limit)


def vspec():
    return pl.BlockSpec(memory_space=pltpu.VMEM)


def sspec():
    return pl.BlockSpec(memory_space=pltpu.SMEM)


def sds(shape, dtype):
    return jax.ShapeDtypeStruct(shape, dtype)


def edge_starts(g):
    first = jnp.where(g % 2 == 0, 12, 0)
    return first, 12 - first


def pack_kernel(
    vel_any, off, wt, route_any, send, vel, out, route_s, count, sems
):
    g = lax.axis_index("gz")
    d = lax.axis_index("xy")
    rows = pl.ds(pl.multiple_of(g * 8, 8), 8)
    load = pltpu.make_async_copy(route_any.at[rows], route_s, sems.at[0])
    bricks = [
        pltpu.make_async_copy(vel_any.at[pl.ds(8 * i, 8)], vel.at[pl.ds(8 * i, 8)], sems.at[1 + i])
        for i in range(4)
    ]
    for copy in [load] + bricks:
        copy.start()
    for i in range(32):
        count[i] = 0
    load.wait()
    row = d // 4
    first = (d % 4) * 32
    x = lax.broadcasted_iota(jnp.int32, (64, 128), 1)
    for r in range(32):
        if r % 8 == 0:
            bricks[r // 8].wait()
        dest = route_s[row, first + r]
        k = count[dest]
        count[dest] = k + 1
        o = off[r]
        v = vel[r].reshape(64, 128)
        moved = jnp.where(x < 128 - o, pltpu.roll(v, (128 - o) % 128, 1), 0.0)
        out[r] = (moved * wt[r]).astype(BF16)
        pltpu.make_async_copy(out.at[r], send.at[dest * CAP + k], sems.at[5]).start()
    pltpu.make_async_copy(out, send.at[pl.ds(0, 32)], sems.at[5]).wait()


def pack(velocity, offset, weight, route):
    anywhere = pl.BlockSpec(memory_space=pl.ANY)
    return pl.pallas_call(
        pack_kernel,
        out_shape=sds((32 * CAP, 64, 128), BF16),
        in_specs=[anywhere, sspec(), sspec(), anywhere],
        out_specs=anywhere,
        scratch_shapes=[
            pltpu.VMEM((32, 8, 8, 128), F32),
            pltpu.VMEM((32, 64, 128), BF16),
            pltpu.SMEM((8, 128), jnp.int32),
            pltpu.SMEM((32,), jnp.int32),
            pltpu.SemaphoreType.DMA((6,)),
        ],
        compiler_params=params(VMEM_ALL),
        name="pack",
    )(velocity, offset, weight, route)


def pair_rows(block):
    n = block.shape[0] // 2
    return jnp.stack(
        [jnp.concatenate([block[2 * i], block[2 * i + 1]], axis=0) for i in range(n)]
    )


def edge_pairs(field, y_even):
    lo = pair_rows(field[:, 0:8, :][:, 0:4])
    hi = pair_rows(field[:, 56:64, :][:, 4:8])
    return jnp.where(y_even, hi, lo), jnp.where(y_even, lo, hi)


def prepare_kernel(route, slot, cond, code, c_a, c_b, m_own):
    g = lax.axis_index("gz")
    d = lax.axis_index("xy")
    rows = pl.ds(pl.multiple_of(g * 8, 8), 8)
    lane = lax.broadcasted_iota(jnp.int32, (8, 128), 1) % 32
    mine = (route[rows, :] == d).astype(jnp.int32)
    upto = mine
    for step in (1, 2, 4, 8, 16):
        upto = upto + jnp.where(lane >= step, pltpu.roll(upto, step, 1), 0)
    rank = upto - mine
    word = jnp.where(mine > 0, (slot[rows, :] + 1) << (5 * rank), 0)
    for step in (1, 2, 4, 8, 16):
        word = word + jnp.where(lane >= step, pltpu.roll(word, step, 1), 0)
    code[...] = word
    z_hi, z_lo = edge_starts(g)
    c_a[...] = cond[pl.ds(z_hi, 4)]
    c_b[...] = cond[pl.ds(z_lo, 4)]
    m_own[0], m_own[1] = edge_pairs(cond, d % 2 == 0)


def prepare(route, slot, cond):
    return pl.pallas_call(
        prepare_kernel,
        out_shape=(
            sds((8, 128), jnp.int32),
            sds((4, 64, 128), F32),
            sds((4, 64, 128), F32),
            sds((2, 8, 8, 128), F32),
        ),
        in_specs=[vspec()] * 3,
        out_specs=(vspec(),) * 4,
        compiler_params=params(),
        name="prepare",
    )(route, slot, cond)


def combine_kernel(recv, code, v, z_a, z_b, y_own):
    g = lax.axis_index("gz")
    d = lax.axis_index("xy")
    v[...] = jnp.zeros_like(v)

    def source(s, carry):
        word = code[s // 4, (s % 4) * 32 + 31]
        for k in range(CAP):
            j = ((word >> (5 * k)) & 31) - 1

            @pl.when(j >= 0)
            def _():
                z0 = pl.multiple_of((j // 8) * 8, 8)
                y0 = pl.multiple_of((j % 8) * 8, 8)
                block = recv[s * CAP + k].astype(F32).reshape(8, 8, 128)
                v[pl.ds(z0, 8), pl.ds(y0, 8), :] += block

        return carry

    lax.fori_loop(0, 32, source, 0, unroll=4)
    z_hi, z_lo = edge_starts(g)
    z_a[...] = v[pl.ds(z_hi, 4)]
    z_b[...] = v[pl.ds(z_lo, 4)]
    y_own[0], y_own[1] = edge_pairs(v, d % 2 == 0)


def combine(recv, code):
    return pl.pallas_call(
        combine_kernel,
        out_shape=(
            sds((16, 64, 128), F32),
            sds((4, 64, 128), F32),
            sds((4, 64, 128), F32),
            sds((2, 8, 8, 128), F32),
        ),
        in_specs=[vspec(), sspec()],
        out_specs=(vspec(),) * 4,
        compiler_params=params(),
        name="combine",
    )(recv, code)


def strips_kernel(y_own, r_a, r_b, y_c, y_d):
    d = lax.axis_index("xy")
    y_even = d % 2 == 0
    y_c[0:8] = y_own[0]
    y_d[0:8] = y_own[1]
    for at, field in ((8, r_a), (10, r_b)):
        y_c[at : at + 2], y_d[at : at + 2] = edge_pairs(field, y_even)


def strips(y_own, r_a, r_b):
    return pl.pallas_call(
        strips_kernel,
        out_shape=(sds((12, 8, 128), F32),) * 2,
        in_specs=[vspec()] * 3,
        out_specs=(vspec(),) * 2,
        compiler_params=params(),
        name="strips",
    )(y_own, r_a, r_b)


def split3(x):
    hi = x.astype(BF16)
    rest = x - hi.astype(F32)
    mid = rest.astype(BF16)
    lo = (rest - mid.astype(F32)).astype(BF16)
    return hi, mid, lo


def band(taps):
    i = lax.broadcasted_iota(jnp.int32, (128, 128), 0)
    j = lax.broadcasted_iota(jnp.int32, (128, 128), 1)
    m = jnp.zeros((128, 128), F32)
    for place, tap in enumerate(taps):
        if tap:
            m = jnp.where(i - j == place - 2, F32(tap), m)
    return m.astype(BF16)


S_TAPS = (1.0, 4.0, 6.0, 4.0, 1.0)
D_TAPS = (1.0, -8.0, 0.0, 8.0, -1.0)
NORM = 1.0 / (16.0 * 16.0 * 12.0)


def smooth5(a):
    return (a[0] + a[4]) + 4.0 * (a[1] + a[3]) + 6.0 * a[2]


def deriv5(a):
    return (a[0] - a[4]) + 8.0 * (a[3] - a[1])


def dot(a, b):
    return jnp.dot(a, b, preferred_element_type=F32)


def fill(ext, field, r_a, r_b, q_c, q_d):
    g = lax.axis_index("gz")
    d = lax.axis_index("xy")
    even = g % 2 == 0
    y_even = d % 2 == 0
    at_a = jnp.where(even, 20, 0)
    at_b = 20 - at_a
    low_in = (g > 0).astype(F32)
    high_in = (g < 7).astype(F32)
    keep_a = jnp.where(even, high_in, low_in)
    keep_b = jnp.where(even, low_in, high_in)
    left_in = (d > 0).astype(F32)
    right_in = (d < 31).astype(F32)
    zeros4 = jnp.zeros((4, 128), F32)
    ext[4:20, 8:72, :] = field[...]
    ext[pl.ds(at_a, 4), 8:72, :] = r_a[...] * keep_a
    ext[pl.ds(at_b, 4), 8:72, :] = r_b[...] * keep_b
    for z in range(24):
        c = q_c[z // 2]
        e = q_d[z // 2]
        lo = jnp.where(y_even, e, c)[4 * (z % 2) : 4 * (z % 2) + 4] * left_in
        hi = jnp.where(y_even, c, e)[4 * (z % 2) : 4 * (z % 2) + 4] * right_in
        if z < 16:
            place, keep = z + 4, 1.0
        elif z < 20:
            place, keep = at_a + (z - 16), keep_a
        else:
            place, keep = at_b + (z - 20), keep_b
        ext[place, 0:8, :] = jnp.concatenate([zeros4, lo * keep], axis=0)
        ext[place, 72:80, :] = jnp.concatenate([hi * keep, zeros4], axis=0)


SHIFTS = (2, 1, 0, -1, -2)


def shifted(a):
    return [pltpu.roll(a, sh % 80, 0) for sh in SHIFTS]


def mix_xy(ext, sx, dx):
    weights = jnp.concatenate([band(S_TAPS), band(D_TAPS)], axis=1)
    twice = jnp.concatenate([weights, weights], axis=0)

    def along_x(i, carry):
        part = pl.ds(i * 12, 12)
        h, m, l = split3(ext[part].reshape(12 * 80, 128))
        both = dot(jnp.concatenate([h, m], axis=1), twice) + dot(l, weights)
        sx[part] = both[:, 0:128].reshape(12, 80, 128)
        dx[part] = both[:, 128:256].reshape(12, 80, 128)
        return carry

    lax.fori_loop(0, 2, along_x, 0)

    def along_y(z, carry):
        ss = shifted(sx[z])
        tt = shifted(dx[z])
        dx[z] = smooth5(tt)
        sx[z] = deriv5(ss)
        ext[z] = smooth5(ss)
        return carry

    lax.fori_loop(0, 24, along_y, 0, unroll=2)


def grad_tile(ext, sx, dx, z, tile):
    gx = smooth5([dx[z + i, tile, :] for i in range(5)])
    gy = smooth5([sx[z + i, tile, :] for i in range(5)])
    gz = deriv5([ext[z + i, tile, :] for i in range(5)])
    return gx, gy, gz


def model_kernel(cond, r_a, r_b, q_c, q_d, gm, ext, sx, dx):
    fill(ext, cond, r_a, r_b, q_c, q_d)
    mix_xy(ext, sx, dx)

    def tiles(t, carry):
        tile = pl.ds(pl.multiple_of(t * 8, 8), 8)
        for z in range(20):
            gx, gy, gz = grad_tile(ext, sx, dx, z, tile)
            gm[0, z, tile, :] = gx
            gm[1, z, tile, :] = gy
            gm[2, z, tile, :] = gz
        return carry

    lax.fori_loop(0, 10, tiles, 0)


def model(cond, r_a, r_b, q_c, q_d):
    return pl.pallas_call(
        model_kernel,
        out_shape=sds((3, 20, 80, 128), F32),
        in_specs=[vspec()] * 5,
        out_specs=vspec(),
        scratch_shapes=[pltpu.VMEM((24, 80, 128), F32)] * 3,
        compiler_params=params(),
        cost_estimate=pl.CostEstimate(flops=200_000_000, bytes_accessed=8_000_000, transcendentals=0),
        name="model",
    )(cond, r_a, r_b, q_c, q_d)


def stencil_kernel(v, r_a, r_b, q_c, q_d, gm, out, total, ext, sx, dx, adj, mid_u, mid_t):
    g = lax.axis_index("gz")
    d = lax.axis_index("xy")
    low_in = (g > 0).astype(F32)
    high_in = (g < 7).astype(F32)
    fill(ext, v, r_a, r_b, q_c, q_d)
    mix_xy(ext, sx, dx)
    row = lax.broadcasted_iota(jnp.int32, (8, 128), 0)

    def cross(t, carry):
        y0 = pl.multiple_of(t * 8, 8)
        y = row + (y0 - 8)
        inside = jnp.where((y >= 0) | (d > 0), NORM, 0.0)
        inside = jnp.where((y < 64) | (d < 31), inside, 0.0)
        tile = pl.ds(y0, 8)
        for z in range(20):
            scale = inside
            if z < 2:
                scale = inside * low_in
            if z >= 18:
                scale = inside * high_in
            mx, my, mz = [gm[i, z, tile, :] * scale for i in range(3)]
            vx, vy, vz = [a * scale for a in grad_tile(ext, sx, dx, z, tile)]
            cx = my * vz - mz * vy
            cy = mz * vx - mx * vz
            cz = mx * vy - my * vx
            adj[0, z, tile, :] = vy * cz - vz * cy
            adj[1, z, tile, :] = vz * cx - vx * cz
            adj[2, z, tile, :] = vx * cy - vy * cx
        return carry

    lax.fori_loop(0, 10, cross, 0)

    def back_yz(z, carry):
        p = smooth5([adj[0, z + i] for i in range(5)])
        q = smooth5([adj[1, z + i] for i in range(5)])
        r = deriv5([adj[2, z + i] for i in range(5)])
        mid_u[z] = smooth5(shifted(p))[8:72]
        mid_t[z] = (deriv5(shifted(q)) + smooth5(shifted(r)))[8:72]
        return carry

    lax.fori_loop(0, 16, back_yz, 0)

    w_s = band(S_TAPS)
    w_d = band(D_TAPS)
    w = jnp.concatenate([w_d, w_s], axis=0)
    total[0:8, :] = jnp.zeros((8, 128), F32)

    def back_x(i, carry):
        part = pl.ds(i * 8, 8)
        us = split3(mid_u[part].reshape(512, 128))
        ts = split3(mid_t[part].reshape(512, 128))
        acc = sum(dot(jnp.concatenate([a, b], axis=1), w) for a, b in zip(us, ts))
        acc = acc * NORM
        out[part] = acc.reshape(8, 64, 128).astype(BF16)
        total[0:8, :] += jnp.sum((acc * acc).reshape(64, 8, 128), axis=0)
        return carry

    lax.fori_loop(0, 2, back_x, 0, unroll=2)
    total[...] = jnp.broadcast_to(jnp.sum(total[0:8, :], axis=0, keepdims=True), (256, 128))


def stencil(v, r_a, r_b, q_c, q_d, gm):
    return pl.pallas_call(
        stencil_kernel,
        out_shape=(sds((16, 64, 128), BF16), sds((256, 128), F32)),
        in_specs=[vspec()] * 6,
        out_specs=(vspec(),) * 2,
        scratch_shapes=[
            pltpu.VMEM((24, 80, 128), F32),
            pltpu.VMEM((24, 80, 128), F32),
            pltpu.VMEM((24, 80, 128), F32),
            pltpu.VMEM((3, 20, 80, 128), F32),
            pltpu.VMEM((16, 64, 128), F32),
            pltpu.VMEM((16, 64, 128), F32),
        ],
        compiler_params=params(),
        name="stencil",
    )(v, r_a, r_b, q_c, q_d, gm)


def scale_kernel(cells, sums, *refs):
    pieces, out = refs[:-1], refs[-1]
    g = lax.axis_index("gz")
    total = jnp.sum(sums[...], axis=0, keepdims=True)
    total = jnp.sum(total, axis=1, keepdims=True)
    scale = 1.0 / jnp.sqrt(total / cells + 1e-06)
    scale = jnp.broadcast_to(scale, (64, 128))
    left, right, across = lax.rem(g + 6, 8), lax.rem(g + 2, 8), lax.rem(g + 4, 8)
    owners = (g, left, right, across, g ^ 1, left ^ 1, right ^ 1, across ^ 1)
    for piece, owner in zip(pieces, owners):
        for z in range(16):
            out[owner * 16 + z] = (piece[z].astype(F32) * scale).astype(BF16)


def scaled(cells, sums, pieces):
    return pl.pallas_call(
        functools.partial(scale_kernel, cells),
        out_shape=sds((128, 64, 128), BF16),
        in_specs=[vspec()] * (1 + len(pieces)),
        out_specs=vspec(),
        compiler_params=params(),
        name="scale",
    )(sums, *pieces)


def swap_odd(count):
    return [(i, (i + 1) % count if i % 2 else (i - 1) % count) for i in range(count)]


def swap_even(count):
    return [(i, i ^ 1) for i in range(count)]


def local(velocity, offset, interp_weight, route, dest_slot, conductivity):
    n_g = lax.axis_size("gz")
    n_x = lax.axis_size("xy")
    z_even, z_odd = swap_even(n_g), swap_odd(n_g)
    y_even, y_odd = swap_even(n_x), swap_odd(n_x)
    route = route.reshape(64, 128)
    send = pack(velocity, offset, interp_weight, route)
    send, route, dest_slot, conductivity = lax.optimization_barrier(
        (send, route, dest_slot, conductivity)
    )
    recv = lax.all_to_all(
        send.reshape(n_x, CAP * 64, 128), "xy", split_axis=0, concat_axis=0, tiled=True
    )
    code, c_a, c_b, m_own = prepare(route, dest_slot.reshape(64, 128), conductivity)
    rc_b = lax.ppermute(c_b, "gz", z_odd)
    rc_a = lax.ppermute(c_a, "gz", z_even)
    m_c, m_d = strips(m_own, rc_a, rc_b)
    qm_c = lax.ppermute(m_c, "xy", y_even)
    qm_d = lax.ppermute(m_d, "xy", y_odd)
    recv, code, qm_c, qm_d = lax.optimization_barrier((recv, code, qm_c, qm_d))
    v, z_a, z_b, y_own = combine(recv.reshape(n_x * CAP, 64, 128), code)
    r_b = lax.ppermute(z_b, "gz", z_odd)
    r_a = lax.ppermute(z_a, "gz", z_even)
    y_c, y_d = strips(y_own, r_a, r_b)
    y_c, y_d, qm_c, qm_d = lax.optimization_barrier((y_c, y_d, qm_c, qm_d))
    q_c = lax.ppermute(y_c, "xy", y_even)
    q_d = lax.ppermute(y_d, "xy", y_odd)
    gm = model(conductivity, rc_a, rc_b, qm_c, qm_d)
    grad, total = stencil(v, r_a, r_b, q_c, q_d, gm)
    core = swap_even(n_g)
    before = lax.ppermute(grad, "gz", [(i, (i + 2) % n_g) for i in range(n_g)])
    after = lax.ppermute(grad, "gz", [(i, (i - 2) % n_g) for i in range(n_g)])
    across = lax.ppermute(grad, "gz", [(i, (i + 4) % n_g) for i in range(n_g)])
    twin = lax.ppermute(grad, "gz", core)
    sums = lax.all_to_all(total, ("gz", "xy"), 0, 0, tiled=True)
    before, after, across, sums = lax.optimization_barrier((before, after, across, sums))
    others = [lax.ppermute(piece, "gz", core) for piece in (before, after, across)]
    pieces = [grad, before, after, across, twin] + others
    cells = float(n_g * n_x * 16 * 64 * 128)
    return scaled(cells, sums, pieces)


def solution(mesh):
    in_specs = (
        P(("gz", "xy"), None, None, None),
        P(("gz", "xy")),
        P(("gz", "xy")),
        P(),
        P(),
        P("gz", "xy", None),
    )
    out_specs = P(None, "xy", None)
    return jax.shard_map(local, mesh=mesh, in_specs=in_specs, out_specs=out_specs, check_vma=False)
```

```python
import functools

import jax
import jax.numpy as jnp
from jax import lax
from jax.experimental import pallas as pl
from jax.experimental.pallas import tpu as pltpu
from jax.sharding import PartitionSpec as P

F32 = jnp.float32
BF16 = jnp.bfloat16
VMEM_LIMIT = 24 * 1024 * 1024
VMEM_ALL = 60 * 1024 * 1024
CAP = 4


def params(limit=VMEM_LIMIT):
    return pltpu.CompilerParams(vmem_limit_bytes=limit)


def vspec():
    return pl.BlockSpec(memory_space=pltpu.VMEM)


def sspec():
    return pl.BlockSpec(memory_space=pltpu.SMEM)


def sds(shape, dtype):
    return jax.ShapeDtypeStruct(shape, dtype)


def edge_starts(g):
    first = jnp.where(g % 2 == 0, 12, 0)
    return first, 12 - first


def pack_kernel(
    vel_any, off, wt, route_any, send, vel, out, route_s, count, sems
):
    g = lax.axis_index("gz")
    d = lax.axis_index("xy")
    rows = pl.ds(pl.multiple_of(g * 8, 8), 8)
    load = pltpu.make_async_copy(route_any.at[rows], route_s, sems.at[0])
    bricks = [
        pltpu.make_async_copy(vel_any.at[pl.ds(8 * i, 8)], vel.at[pl.ds(8 * i, 8)], sems.at[1 + i])
        for i in range(4)
    ]
    for copy in [load] + bricks:
        copy.start()
    for i in range(32):
        count[i] = 0
    load.wait()
    row = d // 4
    first = (d % 4) * 32
    x = lax.broadcasted_iota(jnp.int32, (64, 128), 1)
    for r in range(32):
        if r % 8 == 0:
            bricks[r // 8].wait()
        dest = route_s[row, first + r]
        k = count[dest]
        count[dest] = k + 1
        o = off[r]
        v = vel[r].reshape(64, 128)
        moved = jnp.where(x < 128 - o, pltpu.roll(v, (128 - o) % 128, 1), 0.0)
        out[r] = (moved * wt[r]).astype(BF16)
        pltpu.make_async_copy(out.at[r], send.at[dest * CAP + k], sems.at[5]).start()
    pltpu.make_async_copy(out, send.at[pl.ds(0, 32)], sems.at[5]).wait()


def pack(velocity, offset, weight, route):
    anywhere = pl.BlockSpec(memory_space=pl.ANY)
    return pl.pallas_call(
        pack_kernel,
        out_shape=sds((32 * CAP, 64, 128), BF16),
        in_specs=[anywhere, sspec(), sspec(), anywhere],
        out_specs=anywhere,
        scratch_shapes=[
            pltpu.VMEM((32, 8, 8, 128), F32),
            pltpu.VMEM((32, 64, 128), BF16),
            pltpu.SMEM((8, 128), jnp.int32),
            pltpu.SMEM((32,), jnp.int32),
            pltpu.SemaphoreType.DMA((6,)),
        ],
        compiler_params=params(VMEM_ALL),
        name="pack",
    )(velocity, offset, weight, route)


def pair_rows(block):
    n = block.shape[0] // 2
    return jnp.stack(
        [jnp.concatenate([block[2 * i], block[2 * i + 1]], axis=0) for i in range(n)]
    )


def edge_pairs(field, y_even):
    lo = pair_rows(field[:, 0:8, :][:, 0:4])
    hi = pair_rows(field[:, 56:64, :][:, 4:8])
    return jnp.where(y_even, hi, lo), jnp.where(y_even, lo, hi)


def prepare_kernel(route, slot, cond, code, c_a, c_b, m_own):
    g = lax.axis_index("gz")
    d = lax.axis_index("xy")
    rows = pl.ds(pl.multiple_of(g * 8, 8), 8)
    lane = lax.broadcasted_iota(jnp.int32, (8, 128), 1) % 32
    mine = (route[rows, :] == d).astype(jnp.int32)
    upto = mine
    for step in (1, 2, 4, 8, 16):
        upto = upto + jnp.where(lane >= step, pltpu.roll(upto, step, 1), 0)
    rank = upto - mine
    word = jnp.where(mine > 0, (slot[rows, :] + 1) << (5 * rank), 0)
    for step in (1, 2, 4, 8, 16):
        word = word + jnp.where(lane >= step, pltpu.roll(word, step, 1), 0)
    code[...] = word
    z_hi, z_lo = edge_starts(g)
    c_a[...] = cond[pl.ds(z_hi, 4)]
    c_b[...] = cond[pl.ds(z_lo, 4)]
    m_own[0], m_own[1] = edge_pairs(cond, d % 2 == 0)


def prepare(route, slot, cond):
    return pl.pallas_call(
        prepare_kernel,
        out_shape=(
            sds((8, 128), jnp.int32),
            sds((4, 64, 128), F32),
            sds((4, 64, 128), F32),
            sds((2, 8, 8, 128), F32),
        ),
        in_specs=[vspec()] * 3,
        out_specs=(vspec(),) * 4,
        compiler_params=params(),
        name="prepare",
    )(route, slot, cond)


def lists_kernel(code, count, entries):
    for j in range(16):
        count[j] = 0

    def source(s, carry):
        word = code[s // 4, (s % 4) * 32 + 31]
        for k in range(CAP):
            j = ((word >> (5 * k)) & 31) - 1

            @pl.when(j >= 0)
            def _():
                n = count[j]
                entries[j * 128 + n] = s * CAP + k
                count[j] = n + 1

        return carry

    lax.fori_loop(0, 32, source, 0)


def lists(code):
    return pl.pallas_call(
        lists_kernel,
        out_shape=(sds((16,), jnp.int32), sds((16 * 128,), jnp.int32)),
        in_specs=[sspec()],
        out_specs=(sspec(), sspec()),
        compiler_params=params(),
        name="lists",
    )(code)


def combine_kernel(recv, count, entries, v, z_a, z_b, y_own):
    g = lax.axis_index("gz")
    d = lax.axis_index("xy")
    for j in range(16):

        def record(i, acc):
            return acc + recv[entries[j * 128 + i]].astype(F32)

        block = lax.fori_loop(0, count[j], record, jnp.zeros((64, 128), F32))
        z0, y0 = (j // 8) * 8, (j % 8) * 8
        v[z0 : z0 + 8, y0 : y0 + 8, :] = block.reshape(8, 8, 128)
    z_hi, z_lo = edge_starts(g)
    z_a[...] = v[pl.ds(z_hi, 4)]
    z_b[...] = v[pl.ds(z_lo, 4)]
    y_own[0], y_own[1] = edge_pairs(v, d % 2 == 0)


def combine(recv, count, entries):
    return pl.pallas_call(
        combine_kernel,
        out_shape=(
            sds((16, 64, 128), F32),
            sds((4, 64, 128), F32),
            sds((4, 64, 128), F32),
            sds((2, 8, 8, 128), F32),
        ),
        in_specs=[vspec(), sspec(), sspec()],
        out_specs=(vspec(),) * 4,
        compiler_params=params(),
        name="combine",
    )(recv, count, entries)


def strips_kernel(y_own, r_a, r_b, y_c, y_d):
    d = lax.axis_index("xy")
    y_even = d % 2 == 0
    y_c[0:8] = y_own[0]
    y_d[0:8] = y_own[1]
    for at, field in ((8, r_a), (10, r_b)):
        y_c[at : at + 2], y_d[at : at + 2] = edge_pairs(field, y_even)


def strips(y_own, r_a, r_b):
    return pl.pallas_call(
        strips_kernel,
        out_shape=(sds((12, 8, 128), F32),) * 2,
        in_specs=[vspec()] * 3,
        out_specs=(vspec(),) * 2,
        compiler_params=params(),
        name="strips",
    )(y_own, r_a, r_b)


def split3(x):
    hi = x.astype(BF16)
    rest = x - hi.astype(F32)
    mid = rest.astype(BF16)
    lo = (rest - mid.astype(F32)).astype(BF16)
    return hi, mid, lo


def band(taps):
    i = lax.broadcasted_iota(jnp.int32, (128, 128), 0)
    j = lax.broadcasted_iota(jnp.int32, (128, 128), 1)
    m = jnp.zeros((128, 128), F32)
    for place, tap in enumerate(taps):
        if tap:
            m = jnp.where(i - j == place - 2, F32(tap), m)
    return m.astype(BF16)


S_TAPS = (1.0, 4.0, 6.0, 4.0, 1.0)
D_TAPS = (1.0, -8.0, 0.0, 8.0, -1.0)
NORM = 1.0 / (16.0 * 16.0 * 12.0)


def smooth5(a):
    return (a[0] + a[4]) + 4.0 * (a[1] + a[3]) + 6.0 * a[2]


def deriv5(a):
    return (a[0] - a[4]) + 8.0 * (a[3] - a[1])


def dot(a, b):
    return jnp.dot(a, b, preferred_element_type=F32)


def fill(ext, field, r_a, r_b, q_c, q_d):
    g = lax.axis_index("gz")
    d = lax.axis_index("xy")
    even = g % 2 == 0
    y_even = d % 2 == 0
    at_a = jnp.where(even, 20, 0)
    at_b = 20 - at_a
    low_in = (g > 0).astype(F32)
    high_in = (g < 7).astype(F32)
    keep_a = jnp.where(even, high_in, low_in)
    keep_b = jnp.where(even, low_in, high_in)
    left_in = (d > 0).astype(F32)
    right_in = (d < 31).astype(F32)
    zeros4 = jnp.zeros((4, 128), F32)
    ext[4:20, 8:72, :] = field[...]
    ext[pl.ds(at_a, 4), 8:72, :] = r_a[...] * keep_a
    ext[pl.ds(at_b, 4), 8:72, :] = r_b[...] * keep_b
    for z in range(24):
        c = q_c[z // 2]
        e = q_d[z // 2]
        lo = jnp.where(y_even, e, c)[4 * (z % 2) : 4 * (z % 2) + 4] * left_in
        hi = jnp.where(y_even, c, e)[4 * (z % 2) : 4 * (z % 2) + 4] * right_in
        if z < 16:
            place, keep = z + 4, 1.0
        elif z < 20:
            place, keep = at_a + (z - 16), keep_a
        else:
            place, keep = at_b + (z - 20), keep_b
        ext[place, 0:8, :] = jnp.concatenate([zeros4, lo * keep], axis=0)
        ext[place, 72:80, :] = jnp.concatenate([hi * keep, zeros4], axis=0)


def mix_xy(ext, sx, dx):
    weights = jnp.concatenate([band(S_TAPS), band(D_TAPS)], axis=1)
    twice = jnp.concatenate([weights, weights], axis=0)

    def along_x(i, carry):
        part = pl.ds(i * 12, 12)
        h, m, l = split3(ext[part].reshape(12 * 80, 128))
        both = dot(jnp.concatenate([h, m], axis=1), twice) + dot(l, weights)
        sx[part] = both[:, 0:128].reshape(12, 80, 128)
        dx[part] = both[:, 128:256].reshape(12, 80, 128)
        return carry

    lax.fori_loop(0, 2, along_x, 0)

    def along_y(z, carry):
        ss = [sx[z, 2 + i : 74 + i, :] for i in range(5)]
        tt = [dx[z, 2 + i : 74 + i, :] for i in range(5)]
        yx, xy, yy = smooth5(tt), deriv5(ss), smooth5(ss)
        dx[z, 4:76, :] = yx
        sx[z, 4:76, :] = xy
        ext[z, 4:76, :] = yy
        return carry

    lax.fori_loop(0, 24, along_y, 0, unroll=2)


def grad_tile(ext, sx, dx, z, tile):
    gx = smooth5([dx[z + i, tile, :] for i in range(5)])
    gy = smooth5([sx[z + i, tile, :] for i in range(5)])
    gz = deriv5([ext[z + i, tile, :] for i in range(5)])
    return gx, gy, gz


def model_kernel(cond, r_a, r_b, q_c, q_d, gm, ext, sx, dx):
    fill(ext, cond, r_a, r_b, q_c, q_d)
    mix_xy(ext, sx, dx)

    def tiles(t, carry):
        tile = pl.ds(pl.multiple_of(t * 8, 8), 8)
        for z in range(20):
            gx, gy, gz = grad_tile(ext, sx, dx, z, tile)
            gm[0, z, tile, :] = gx
            gm[1, z, tile, :] = gy
            gm[2, z, tile, :] = gz
        return carry

    lax.fori_loop(0, 10, tiles, 0)


def model(cond, r_a, r_b, q_c, q_d):
    return pl.pallas_call(
        model_kernel,
        out_shape=sds((3, 20, 80, 128), F32),
        in_specs=[vspec()] * 5,
        out_specs=vspec(),
        scratch_shapes=[pltpu.VMEM((24, 80, 128), F32)] * 3,
        compiler_params=params(),
        cost_estimate=pl.CostEstimate(flops=200_000_000, bytes_accessed=8_000_000, transcendentals=0),
        name="model",
    )(cond, r_a, r_b, q_c, q_d)


def stencil_kernel(v, r_a, r_b, q_c, q_d, gm, out, total, ext, sx, dx, back):
    g = lax.axis_index("gz")
    d = lax.axis_index("xy")
    low_in = (g > 0).astype(F32)
    high_in = (g < 7).astype(F32)
    fill(ext, v, r_a, r_b, q_c, q_d)
    mix_xy(ext, sx, dx)
    row = lax.broadcasted_iota(jnp.int32, (8, 128), 0)

    def cross(t, carry):
        y0 = pl.multiple_of(t * 8, 8)
        y = row + (y0 - 8)
        inside = jnp.where((y >= 0) | (d > 0), NORM, 0.0)
        inside = jnp.where((y < 64) | (d < 31), inside, 0.0)
        tile = pl.ds(y0, 8)
        adj = []
        for z in range(20):
            scale = inside
            if z < 2:
                scale = inside * low_in
            if z >= 18:
                scale = inside * high_in
            mx, my, mz = [gm[i, z, tile, :] * scale for i in range(3)]
            vx, vy, vz = [a * scale for a in grad_tile(ext, sx, dx, z, tile)]
            cx = my * vz - mz * vy
            cy = mz * vx - mx * vz
            cz = mx * vy - my * vx
            adj.append((vy * cz - vz * cy, vz * cx - vx * cz, vx * cy - vy * cx))
            if z >= 4:
                ax, ay, az = zip(*adj[z - 4 :])
                back[0, z - 4, tile, :] = smooth5(ax)
                back[1, z - 4, tile, :] = smooth5(ay)
                back[2, z - 4, tile, :] = deriv5(az)
        return carry

    lax.fori_loop(0, 10, cross, 0)

    w_s = band(S_TAPS)
    w_d = band(D_TAPS)
    w = jnp.concatenate([w_d, w_s], axis=0)
    total[0:8, :] = jnp.zeros((8, 128), F32)

    w = jnp.concatenate([w, w, w], axis=0)

    def back_xy(i, carry):
        part = pl.ds(i * 8, 8)
        p, q, r = [[back[j, part, 6 + k : 70 + k, :] for k in range(5)] for j in range(3)]
        us = split3(smooth5(p).reshape(512, 128))
        ts = split3((deriv5(q) + smooth5(r)).reshape(512, 128))
        both = [x for pair in zip(us, ts) for x in pair]
        acc = dot(jnp.concatenate(both, axis=1), w) * NORM
        out[part] = acc.reshape(8, 64, 128).astype(BF16)
        total[0:8, :] += jnp.sum((acc * acc).reshape(64, 8, 128), axis=0)
        return carry

    lax.fori_loop(0, 2, back_xy, 0, unroll=2)
    total[...] = jnp.broadcast_to(jnp.sum(total[0:8, :], axis=0, keepdims=True), (256, 128))


def stencil(v, r_a, r_b, q_c, q_d, gm):
    return pl.pallas_call(
        stencil_kernel,
        out_shape=(sds((16, 64, 128), BF16), sds((256, 128), F32)),
        in_specs=[vspec()] * 6,
        out_specs=(vspec(),) * 2,
        scratch_shapes=[
            pltpu.VMEM((24, 80, 128), F32),
            pltpu.VMEM((24, 80, 128), F32),
            pltpu.VMEM((24, 80, 128), F32),
            pltpu.VMEM((3, 16, 80, 128), F32),
        ],
        compiler_params=params(),
        name="stencil",
    )(v, r_a, r_b, q_c, q_d, gm)


def scale_kernel(cells, sums, *refs):
    pieces, out, held, sems = refs[:-3], refs[-3], refs[-2], refs[-1]
    g = lax.axis_index("gz")
    total = jnp.sum(sums[...], axis=0, keepdims=True)
    total = jnp.sum(total, axis=1, keepdims=True)
    scale = 1.0 / jnp.sqrt(total / cells + 1e-06)
    scale = jnp.broadcast_to(scale, (64, 128))
    left, right, across = lax.rem(g + 6, 8), lax.rem(g + 2, 8), lax.rem(g + 4, 8)
    owners = (g, left, right, across, g ^ 1, left ^ 1, right ^ 1, across ^ 1)
    copies = []
    for k, (piece, owner) in enumerate(zip(pieces, owners)):
        for z in range(16):
            held[k, z] = (piece[z].astype(F32) * scale).astype(BF16)
        copy = pltpu.make_async_copy(held.at[k], out.at[pl.ds(owner * 16, 16)], sems.at[k])
        copy.start()
        copies.append(copy)
    for copy in copies:
        copy.wait()


def scaled(cells, sums, pieces):
    return pl.pallas_call(
        functools.partial(scale_kernel, cells),
        out_shape=sds((128, 64, 128), BF16),
        in_specs=[vspec()] * (1 + len(pieces)),
        out_specs=pl.BlockSpec(memory_space=pl.ANY),
        scratch_shapes=[pltpu.VMEM((8, 16, 64, 128), BF16), pltpu.SemaphoreType.DMA((8,))],
        compiler_params=params(),
        name="scale",
    )(sums, *pieces)


def swap_odd(count):
    return [(i, (i + 1) % count if i % 2 else (i - 1) % count) for i in range(count)]


def swap_even(count):
    return [(i, i ^ 1) for i in range(count)]


def local(velocity, offset, interp_weight, route, dest_slot, conductivity):
    n_g = lax.axis_size("gz")
    n_x = lax.axis_size("xy")
    z_even, z_odd = swap_even(n_g), swap_odd(n_g)
    y_even, y_odd = swap_even(n_x), swap_odd(n_x)
    route = route.reshape(64, 128)
    send = pack(velocity, offset, interp_weight, route)
    send, route, dest_slot, conductivity = lax.optimization_barrier(
        (send, route, dest_slot, conductivity)
    )
    recv = lax.all_to_all(
        send.reshape(n_x, CAP * 64, 128), "xy", split_axis=0, concat_axis=0, tiled=True
    )
    code, c_a, c_b, m_own = prepare(route, dest_slot.reshape(64, 128), conductivity)
    rc_b = lax.ppermute(c_b, "gz", z_odd)
    rc_a = lax.ppermute(c_a, "gz", z_even)
    m_c, m_d = strips(m_own, rc_a, rc_b)
    qm_c = lax.ppermute(m_c, "xy", y_even)
    qm_d = lax.ppermute(m_d, "xy", y_odd)
    count, entries = lists(code)
    recv, count, entries, qm_c, qm_d = lax.optimization_barrier((recv, count, entries, qm_c, qm_d))
    v, z_a, z_b, y_own = combine(recv.reshape(n_x * CAP, 64, 128), count, entries)
    z_a, z_b, qm_c, qm_d = lax.optimization_barrier((z_a, z_b, qm_c, qm_d))
    r_b = lax.ppermute(z_b, "gz", z_odd)
    r_a = lax.ppermute(z_a, "gz", z_even)
    gm = model(conductivity, rc_a, rc_b, qm_c, qm_d)
    y_c, y_d = strips(y_own, r_a, r_b)
    q_c = lax.ppermute(y_c, "xy", y_even)
    q_d = lax.ppermute(y_d, "xy", y_odd)
    grad, total = stencil(v, r_a, r_b, q_c, q_d, gm)
    core = swap_even(n_g)
    before = lax.ppermute(grad, "gz", [(i, (i + 2) % n_g) for i in range(n_g)])
    after = lax.ppermute(grad, "gz", [(i, (i - 2) % n_g) for i in range(n_g)])
    across = lax.ppermute(grad, "gz", [(i, (i + 4) % n_g) for i in range(n_g)])
    twin = lax.ppermute(grad, "gz", core)
    sums = lax.all_to_all(total, ("gz", "xy"), 0, 0, tiled=True)
    before, after, across, sums = lax.optimization_barrier((before, after, across, sums))
    others = [lax.ppermute(piece, "gz", core) for piece in (before, after, across)]
    pieces = [grad, before, after, across, twin] + others
    cells = float(n_g * n_x * 16 * 64 * 128)
    return scaled(cells, sums, pieces)


def solution(mesh):
    in_specs = (
        P(("gz", "xy"), None, None, None),
        P(("gz", "xy")),
        P(("gz", "xy")),
        P(),
        P(),
        P("gz", "xy", None),
    )
    out_specs = P(None, "xy", None)
    return jax.shard_map(local, mesh=mesh, in_specs=in_specs, out_specs=out_specs, check_vma=False)
```

```python
import functools

import jax
import jax.numpy as jnp
from jax import lax
from jax.experimental import pallas as pl
from jax.experimental.pallas import tpu as pltpu
from jax.sharding import PartitionSpec as P

F32 = jnp.float32
BF16 = jnp.bfloat16
VMEM_LIMIT = 24 * 1024 * 1024
VMEM_ALL = 60 * 1024 * 1024
CAP = 4


def params(limit=VMEM_LIMIT):
    return pltpu.CompilerParams(vmem_limit_bytes=limit)


def vspec():
    return pl.BlockSpec(memory_space=pltpu.VMEM)


def sspec():
    return pl.BlockSpec(memory_space=pltpu.SMEM)


def sds(shape, dtype):
    return jax.ShapeDtypeStruct(shape, dtype)


def edge_starts(g):
    first = jnp.where(g % 2 == 0, 12, 0)
    return first, 12 - first


def pack_kernel(
    vel_any, off, wt, route_any, send, vel, out, route_s, count, sems
):
    g = lax.axis_index("gz")
    d = lax.axis_index("xy")
    rows = pl.ds(pl.multiple_of(g * 8, 8), 8)
    load = pltpu.make_async_copy(route_any.at[rows], route_s, sems.at[0])
    bricks = [
        pltpu.make_async_copy(vel_any.at[pl.ds(8 * i, 8)], vel.at[pl.ds(8 * i, 8)], sems.at[1 + i])
        for i in range(4)
    ]
    for copy in [load] + bricks:
        copy.start()
    for i in range(32):
        count[i] = 0
    load.wait()
    row = d // 4
    first = (d % 4) * 32
    x = lax.broadcasted_iota(jnp.int32, (64, 128), 1)
    for r in range(32):
        if r % 8 == 0:
            bricks[r // 8].wait()
        dest = route_s[row, first + r]
        k = count[dest]
        count[dest] = k + 1
        o = off[r]
        v = vel[r].reshape(64, 128)
        moved = jnp.where(x < 128 - o, pltpu.roll(v, (128 - o) % 128, 1), 0.0)
        out[r] = (moved * wt[r]).astype(BF16)
        pltpu.make_async_copy(out.at[r], send.at[dest * CAP + k], sems.at[5]).start()
    pltpu.make_async_copy(out, send.at[pl.ds(0, 32)], sems.at[5]).wait()


def pack(velocity, offset, weight, route):
    anywhere = pl.BlockSpec(memory_space=pl.ANY)
    return pl.pallas_call(
        pack_kernel,
        out_shape=sds((32 * CAP, 64, 128), BF16),
        in_specs=[anywhere, sspec(), sspec(), anywhere],
        out_specs=anywhere,
        scratch_shapes=[
            pltpu.VMEM((32, 8, 8, 128), F32),
            pltpu.VMEM((32, 64, 128), BF16),
            pltpu.SMEM((8, 128), jnp.int32),
            pltpu.SMEM((32,), jnp.int32),
            pltpu.SemaphoreType.DMA((6,)),
        ],
        compiler_params=params(VMEM_ALL),
        name="pack",
    )(velocity, offset, weight, route)


def pair_rows(block):
    n = block.shape[0] // 2
    return jnp.stack(
        [jnp.concatenate([block[2 * i], block[2 * i + 1]], axis=0) for i in range(n)]
    )


def edge_pairs(field, y_even):
    lo = pair_rows(field[:, 0:8, :][:, 0:4])
    hi = pair_rows(field[:, 56:64, :][:, 4:8])
    return jnp.where(y_even, hi, lo), jnp.where(y_even, lo, hi)


def prepare_kernel(route, slot, cond, code, c_a, c_b, m_own):
    g = lax.axis_index("gz")
    d = lax.axis_index("xy")
    rows = pl.ds(pl.multiple_of(g * 8, 8), 8)
    lane = lax.broadcasted_iota(jnp.int32, (8, 128), 1) % 32
    mine = (route[rows, :] == d).astype(jnp.int32)
    upto = mine
    for step in (1, 2, 4, 8, 16):
        upto = upto + jnp.where(lane >= step, pltpu.roll(upto, step, 1), 0)
    rank = upto - mine
    word = jnp.where(mine > 0, (slot[rows, :] + 1) << (5 * rank), 0)
    for step in (1, 2, 4, 8, 16):
        word = word + jnp.where(lane >= step, pltpu.roll(word, step, 1), 0)
    code[...] = word
    z_hi, z_lo = edge_starts(g)
    c_a[...] = cond[pl.ds(z_hi, 4)]
    c_b[...] = cond[pl.ds(z_lo, 4)]
    m_own[0], m_own[1] = edge_pairs(cond, d % 2 == 0)


def prepare(route, slot, cond):
    return pl.pallas_call(
        prepare_kernel,
        out_shape=(
            sds((8, 128), jnp.int32),
            sds((4, 64, 128), F32),
            sds((4, 64, 128), F32),
            sds((2, 8, 8, 128), F32),
        ),
        in_specs=[vspec()] * 3,
        out_specs=(vspec(),) * 4,
        compiler_params=params(),
        name="prepare",
    )(route, slot, cond)


def lists_kernel(code, count, entries):
    for j in range(16):
        count[j] = 0

    def source(s, carry):
        word = code[s // 4, (s % 4) * 32 + 31]
        for k in range(CAP):
            j = ((word >> (5 * k)) & 31) - 1

            @pl.when(j >= 0)
            def _():
                n = count[j]
                entries[j * 128 + n] = s * CAP + k
                count[j] = n + 1

        return carry

    lax.fori_loop(0, 32, source, 0)


def lists(code):
    return pl.pallas_call(
        lists_kernel,
        out_shape=(sds((16,), jnp.int32), sds((16 * 128,), jnp.int32)),
        in_specs=[sspec()],
        out_specs=(sspec(), sspec()),
        compiler_params=params(),
        name="lists",
    )(code)


def combine_kernel(recv, count, entries, v, z_a, z_b, y_c, y_d):
    g = lax.axis_index("gz")
    d = lax.axis_index("xy")
    for j in range(16):

        def record(i, acc):
            return acc + recv[entries[j * 128 + i]].astype(F32)

        block = lax.fori_loop(0, count[j], record, jnp.zeros((64, 128), F32))
        z0, y0 = (j // 8) * 8, (j % 8) * 8
        v[z0 : z0 + 8, y0 : y0 + 8, :] = block.reshape(8, 8, 128)
    z_hi, z_lo = edge_starts(g)
    z_a[...] = v[pl.ds(z_hi, 4)]
    z_b[...] = v[pl.ds(z_lo, 4)]
    y_c[...], y_d[...] = edge_pairs(v, d % 2 == 0)


def combine(recv, count, entries):
    return pl.pallas_call(
        combine_kernel,
        out_shape=(
            sds((16, 64, 128), F32),
            sds((4, 64, 128), F32),
            sds((4, 64, 128), F32),
            sds((8, 8, 128), F32),
            sds((8, 8, 128), F32),
        ),
        in_specs=[vspec(), sspec(), sspec()],
        out_specs=(vspec(),) * 5,
        compiler_params=params(),
        name="combine",
    )(recv, count, entries)


def strips_kernel(y_own, r_a, r_b, y_c, y_d):
    d = lax.axis_index("xy")
    y_even = d % 2 == 0
    y_c[0:8] = y_own[0]
    y_d[0:8] = y_own[1]
    for at, field in ((8, r_a), (10, r_b)):
        y_c[at : at + 2], y_d[at : at + 2] = edge_pairs(field, y_even)


def strips(y_own, r_a, r_b):
    return pl.pallas_call(
        strips_kernel,
        out_shape=(sds((12, 8, 128), F32),) * 2,
        in_specs=[vspec()] * 3,
        out_specs=(vspec(),) * 2,
        compiler_params=params(),
        name="strips",
    )(y_own, r_a, r_b)


def corners_kernel(r_a, r_b, k_c, k_d):
    d = lax.axis_index("xy")
    y_even = d % 2 == 0
    for at, field in ((0, r_a), (2, r_b)):
        k_c[at : at + 2], k_d[at : at + 2] = edge_pairs(field, y_even)


def corners(r_a, r_b):
    return pl.pallas_call(
        corners_kernel,
        out_shape=(sds((4, 8, 128), F32),) * 2,
        in_specs=[vspec()] * 2,
        out_specs=(vspec(),) * 2,
        compiler_params=params(),
        name="corners",
    )(r_a, r_b)


def split3(x):
    hi = x.astype(BF16)
    rest = x - hi.astype(F32)
    mid = rest.astype(BF16)
    lo = (rest - mid.astype(F32)).astype(BF16)
    return hi, mid, lo


def band(taps):
    i = lax.broadcasted_iota(jnp.int32, (128, 128), 0)
    j = lax.broadcasted_iota(jnp.int32, (128, 128), 1)
    m = jnp.zeros((128, 128), F32)
    for place, tap in enumerate(taps):
        if tap:
            m = jnp.where(i - j == place - 2, F32(tap), m)
    return m.astype(BF16)


S_TAPS = (1.0, 4.0, 6.0, 4.0, 1.0)
D_TAPS = (1.0, -8.0, 0.0, 8.0, -1.0)
NORM = 1.0 / (16.0 * 16.0 * 12.0)


def smooth5(a):
    return (a[0] + a[4]) + 4.0 * (a[1] + a[3]) + 6.0 * a[2]


def deriv5(a):
    return (a[0] - a[4]) + 8.0 * (a[3] - a[1])


def dot(a, b):
    return jnp.dot(a, b, preferred_element_type=F32)


def fill(ext, field, r_a, r_b, q_c, q_d, k_c=None, k_d=None):
    g = lax.axis_index("gz")
    d = lax.axis_index("xy")
    even = g % 2 == 0
    y_even = d % 2 == 0
    at_a = jnp.where(even, 20, 0)
    at_b = 20 - at_a
    low_in = (g > 0).astype(F32)
    high_in = (g < 7).astype(F32)
    keep_a = jnp.where(even, high_in, low_in)
    keep_b = jnp.where(even, low_in, high_in)
    left_in = (d > 0).astype(F32)
    right_in = (d < 31).astype(F32)
    zeros4 = jnp.zeros((4, 128), F32)
    ext[4:20, 8:72, :] = field[...]
    ext[pl.ds(at_a, 4), 8:72, :] = r_a[...] * keep_a
    ext[pl.ds(at_b, 4), 8:72, :] = r_b[...] * keep_b
    for z in range(24):
        if k_c is None or z < 16:
            c, e = q_c[z // 2], q_d[z // 2]
        else:
            c, e = k_c[z // 2 - 8], k_d[z // 2 - 8]
        lo = jnp.where(y_even, e, c)[4 * (z % 2) : 4 * (z % 2) + 4] * left_in
        hi = jnp.where(y_even, c, e)[4 * (z % 2) : 4 * (z % 2) + 4] * right_in
        if z < 16:
            place, keep = z + 4, 1.0
        elif z < 20:
            place, keep = at_a + (z - 16), keep_a
        else:
            place, keep = at_b + (z - 20), keep_b
        ext[place, 0:8, :] = jnp.concatenate([zeros4, lo * keep], axis=0)
        ext[place, 72:80, :] = jnp.concatenate([hi * keep, zeros4], axis=0)


def mix_xy(ext, sx, dx):
    weights = jnp.concatenate([band(S_TAPS), band(D_TAPS)], axis=1)
    twice = jnp.concatenate([weights, weights], axis=0)

    def along_x(i, carry):
        part = pl.ds(i * 6, 6)
        h, m, l = split3(ext[part].reshape(6 * 80, 128))
        both = dot(jnp.concatenate([h, m], axis=1), twice) + dot(l, weights)
        sx[part] = both[:, 0:128].reshape(6, 80, 128)
        dx[part] = both[:, 128:256].reshape(6, 80, 128)
        return carry

    lax.fori_loop(0, 4, along_x, 0, unroll=4)

    def along_y(z, carry):
        ss = [sx[z, 2 + i : 74 + i, :] for i in range(5)]
        tt = [dx[z, 2 + i : 74 + i, :] for i in range(5)]
        yx, xy, yy = smooth5(tt), deriv5(ss), smooth5(ss)
        dx[z, 4:76, :] = yx
        sx[z, 4:76, :] = xy
        ext[z, 4:76, :] = yy
        return carry

    lax.fori_loop(0, 24, along_y, 0, unroll=4)


def grad_tile(ext, sx, dx, z, tile):
    gx = smooth5([dx[z + i, tile, :] for i in range(5)])
    gy = smooth5([sx[z + i, tile, :] for i in range(5)])
    gz = deriv5([ext[z + i, tile, :] for i in range(5)])
    return gx, gy, gz


def model_kernel(cond, r_a, r_b, q_c, q_d, gm, ext, sx, dx):
    fill(ext, cond, r_a, r_b, q_c, q_d)
    mix_xy(ext, sx, dx)

    def tiles(t, carry):
        tile = pl.ds(pl.multiple_of(t * 8, 8), 8)
        for z in range(20):
            gx, gy, gz = grad_tile(ext, sx, dx, z, tile)
            gm[0, z, tile, :] = gx
            gm[1, z, tile, :] = gy
            gm[2, z, tile, :] = gz
        return carry

    lax.fori_loop(0, 10, tiles, 0)


def model(cond, r_a, r_b, q_c, q_d):
    return pl.pallas_call(
        model_kernel,
        out_shape=sds((3, 20, 80, 128), F32),
        in_specs=[vspec()] * 5,
        out_specs=vspec(),
        scratch_shapes=[pltpu.VMEM((24, 80, 128), F32)] * 3,
        compiler_params=params(),
        cost_estimate=pl.CostEstimate(flops=200_000_000, bytes_accessed=8_000_000, transcendentals=0),
        name="model",
    )(cond, r_a, r_b, q_c, q_d)


def stencil_kernel(v, r_a, r_b, q_c, q_d, k_c, k_d, gm, out, total, ext, sx, dx, back):
    g = lax.axis_index("gz")
    d = lax.axis_index("xy")
    low_in = (g > 0).astype(F32)
    high_in = (g < 7).astype(F32)
    fill(ext, v, r_a, r_b, q_c, q_d, k_c, k_d)
    mix_xy(ext, sx, dx)
    row = lax.broadcasted_iota(jnp.int32, (8, 128), 0)

    def cross(t, carry):
        y0 = pl.multiple_of(t * 8, 8)
        y = row + (y0 - 8)
        inside = jnp.where((y >= 0) | (d > 0), NORM, 0.0)
        inside = jnp.where((y < 64) | (d < 31), inside, 0.0)
        tile = pl.ds(y0, 8)
        adj = []
        for z in range(20):
            scale = inside
            if z < 2:
                scale = inside * low_in
            if z >= 18:
                scale = inside * high_in
            mx, my, mz = [gm[i, z, tile, :] * scale for i in range(3)]
            vx, vy, vz = [a * scale for a in grad_tile(ext, sx, dx, z, tile)]
            cx = my * vz - mz * vy
            cy = mz * vx - mx * vz
            cz = mx * vy - my * vx
            adj.append((vy * cz - vz * cy, vz * cx - vx * cz, vx * cy - vy * cx))
            if z >= 4:
                ax, ay, az = zip(*adj[z - 4 :])
                back[0, z - 4, tile, :] = smooth5(ax)
                back[1, z - 4, tile, :] = smooth5(ay)
                back[2, z - 4, tile, :] = deriv5(az)
        return carry

    lax.fori_loop(0, 10, cross, 0)

    w_s = band(S_TAPS)
    w_d = band(D_TAPS)
    w = jnp.concatenate([w_d, w_s], axis=0)

    w = jnp.concatenate([w, w, w], axis=0)

    p, q, r = [[back[j, :, 6 + k : 70 + k, :] for k in range(5)] for j in range(3)]
    us = split3(smooth5(p).reshape(1024, 128))
    ts = split3((deriv5(q) + smooth5(r)).reshape(1024, 128))
    both = [x for pair in zip(us, ts) for x in pair]
    acc = dot(jnp.concatenate(both, axis=1), w) * NORM
    out[...] = acc.reshape(16, 64, 128).astype(BF16)
    squares = jnp.sum((acc * acc).reshape(128, 8, 128), axis=0)
    total[...] = jnp.broadcast_to(jnp.sum(squares, axis=0, keepdims=True), (256, 128))


def stencil(v, r_a, r_b, q_c, q_d, k_c, k_d, gm):
    return pl.pallas_call(
        stencil_kernel,
        out_shape=(sds((16, 64, 128), BF16), sds((256, 128), F32)),
        in_specs=[vspec()] * 8,
        out_specs=(vspec(),) * 2,
        scratch_shapes=[
            pltpu.VMEM((24, 80, 128), F32),
            pltpu.VMEM((24, 80, 128), F32),
            pltpu.VMEM((24, 80, 128), F32),
            pltpu.VMEM((3, 16, 80, 128), F32),
        ],
        compiler_params=params(),
        name="stencil",
    )(v, r_a, r_b, q_c, q_d, k_c, k_d, gm)


def scale_kernel(cells, sums, *refs):
    pieces, out, held, sems = refs[:-3], refs[-3], refs[-2], refs[-1]
    g = lax.axis_index("gz")
    total = jnp.sum(sums[...], axis=0, keepdims=True)
    total = jnp.sum(total, axis=1, keepdims=True)
    scale = 1.0 / jnp.sqrt(total / cells + 1e-06)
    scale = jnp.broadcast_to(scale, (64, 128))
    left, right, across = lax.rem(g + 6, 8), lax.rem(g + 2, 8), lax.rem(g + 4, 8)
    owners = (g, left, right, across, g ^ 1, left ^ 1, right ^ 1, across ^ 1)
    copies = []
    for k, (piece, owner) in enumerate(zip(pieces, owners)):
        for z in range(16):
            held[k, z] = (piece[z].astype(F32) * scale).astype(BF16)
        copy = pltpu.make_async_copy(held.at[k], out.at[pl.ds(owner * 16, 16)], sems.at[k])
        copy.start()
        copies.append(copy)
    for copy in copies:
        copy.wait()


def scaled(cells, sums, pieces):
    return pl.pallas_call(
        functools.partial(scale_kernel, cells),
        out_shape=sds((128, 64, 128), BF16),
        in_specs=[vspec()] * (1 + len(pieces)),
        out_specs=pl.BlockSpec(memory_space=pl.ANY),
        scratch_shapes=[pltpu.VMEM((8, 16, 64, 128), BF16), pltpu.SemaphoreType.DMA((8,))],
        compiler_params=params(),
        name="scale",
    )(sums, *pieces)


def swap_odd(count):
    return [(i, (i + 1) % count if i % 2 else (i - 1) % count) for i in range(count)]


def swap_even(count):
    return [(i, i ^ 1) for i in range(count)]


def local(velocity, offset, interp_weight, route, dest_slot, conductivity):
    n_g = lax.axis_size("gz")
    n_x = lax.axis_size("xy")
    z_even, z_odd = swap_even(n_g), swap_odd(n_g)
    y_even, y_odd = swap_even(n_x), swap_odd(n_x)
    route = route.reshape(64, 128)
    send = pack(velocity, offset, interp_weight, route)
    send, route, dest_slot, conductivity = lax.optimization_barrier(
        (send, route, dest_slot, conductivity)
    )
    recv = lax.all_to_all(
        send.reshape(n_x, CAP * 64, 128), "xy", split_axis=0, concat_axis=0, tiled=True
    )
    code, c_a, c_b, m_own = prepare(route, dest_slot.reshape(64, 128), conductivity)
    rc_b = lax.ppermute(c_b, "gz", z_odd)
    rc_a = lax.ppermute(c_a, "gz", z_even)
    m_c, m_d = strips(m_own, rc_a, rc_b)
    qm_c = lax.ppermute(m_c, "xy", y_even)
    qm_d = lax.ppermute(m_d, "xy", y_odd)
    count, entries = lists(code)
    recv, count, entries, qm_c, qm_d = lax.optimization_barrier((recv, count, entries, qm_c, qm_d))
    v, z_a, z_b, y_c, y_d = combine(recv.reshape(n_x * CAP, 64, 128), count, entries)
    z_a, z_b, y_c, y_d, qm_c, qm_d = lax.optimization_barrier((z_a, z_b, y_c, y_d, qm_c, qm_d))
    r_b = lax.ppermute(z_b, "gz", z_odd)
    r_a = lax.ppermute(z_a, "gz", z_even)
    q_c = lax.ppermute(y_c, "xy", y_even)
    q_d = lax.ppermute(y_d, "xy", y_odd)
    gm = model(conductivity, rc_a, rc_b, qm_c, qm_d)
    k_c, k_d = corners(r_a, r_b)
    k_c = lax.ppermute(k_c, "xy", y_even)
    k_d = lax.ppermute(k_d, "xy", y_odd)
    grad, total = stencil(v, r_a, r_b, q_c, q_d, k_c, k_d, gm)
    core = swap_even(n_g)
    before = lax.ppermute(grad, "gz", [(i, (i + 2) % n_g) for i in range(n_g)])
    after = lax.ppermute(grad, "gz", [(i, (i - 2) % n_g) for i in range(n_g)])
    across = lax.ppermute(grad, "gz", [(i, (i + 4) % n_g) for i in range(n_g)])
    twin = lax.ppermute(grad, "gz", core)
    sums = lax.all_to_all(total, ("gz", "xy"), 0, 0, tiled=True)
    before, after, across, sums = lax.optimization_barrier((before, after, across, sums))
    others = [lax.ppermute(piece, "gz", core) for piece in (before, after, across)]
    pieces = [grad, before, after, across, twin] + others
    cells = float(n_g * n_x * 16 * 64 * 128)
    return scaled(cells, sums, pieces)


def solution(mesh):
    in_specs = (
        P(("gz", "xy"), None, None, None),
        P(("gz", "xy")),
        P(("gz", "xy")),
        P(),
        P(),
        P("gz", "xy", None),
    )
    out_specs = P(None, "xy", None)
    return jax.shard_map(local, mesh=mesh, in_specs=in_specs, out_specs=out_specs, check_vma=False)
```

```python
import functools

import jax
import jax.numpy as jnp
from jax import lax
from jax.experimental import pallas as pl
from jax.experimental.pallas import tpu as pltpu
from jax.sharding import PartitionSpec as P

F32 = jnp.float32
BF16 = jnp.bfloat16
VMEM_LIMIT = 24 * 1024 * 1024
VMEM_ALL = 60 * 1024 * 1024
CAP = 4


def params(limit=VMEM_LIMIT):
    return pltpu.CompilerParams(vmem_limit_bytes=limit)


def vspec():
    return pl.BlockSpec(memory_space=pltpu.VMEM)


def sspec():
    return pl.BlockSpec(memory_space=pltpu.SMEM)


def sds(shape, dtype):
    return jax.ShapeDtypeStruct(shape, dtype)


def edge_starts(g):
    first = jnp.where(g % 2 == 0, 12, 0)
    return first, 12 - first


def pack_kernel(
    vel_any, off, wt, route_any, send, vel, out, route_s, count, sems
):
    g = lax.axis_index("gz")
    d = lax.axis_index("xy")
    rows = pl.ds(pl.multiple_of(g * 8, 8), 8)
    load = pltpu.make_async_copy(route_any.at[rows], route_s, sems.at[0])
    bricks = [
        pltpu.make_async_copy(vel_any.at[pl.ds(8 * i, 8)], vel.at[pl.ds(8 * i, 8)], sems.at[1 + i])
        for i in range(4)
    ]
    for copy in [load] + bricks:
        copy.start()
    for i in range(32):
        count[i] = 0
    load.wait()
    row = d // 4
    first = (d % 4) * 32
    x = lax.broadcasted_iota(jnp.int32, (64, 128), 1)
    for r in range(32):
        if r % 8 == 0:
            bricks[r // 8].wait()
        dest = route_s[row, first + r]
        k = count[dest]
        count[dest] = k + 1
        o = off[r]
        v = vel[r].reshape(64, 128)
        moved = jnp.where(x < 128 - o, pltpu.roll(v, (128 - o) % 128, 1), 0.0)
        out[r] = (moved * wt[r]).astype(BF16)
        pltpu.make_async_copy(out.at[r], send.at[dest * CAP + k], sems.at[5]).start()
    pltpu.make_async_copy(out, send.at[pl.ds(0, 32)], sems.at[5]).wait()


def pack(velocity, offset, weight, route):
    anywhere = pl.BlockSpec(memory_space=pl.ANY)
    return pl.pallas_call(
        pack_kernel,
        out_shape=sds((32 * CAP, 64, 128), BF16),
        in_specs=[anywhere, sspec(), sspec(), anywhere],
        out_specs=anywhere,
        scratch_shapes=[
            pltpu.VMEM((32, 8, 8, 128), F32),
            pltpu.VMEM((32, 64, 128), BF16),
            pltpu.SMEM((8, 128), jnp.int32),
            pltpu.SMEM((32,), jnp.int32),
            pltpu.SemaphoreType.DMA((6,)),
        ],
        compiler_params=params(VMEM_ALL),
        name="pack",
    )(velocity, offset, weight, route)


def pair_rows(block):
    n = block.shape[0] // 2
    return jnp.stack(
        [jnp.concatenate([block[2 * i], block[2 * i + 1]], axis=0) for i in range(n)]
    )


def edge_pairs(field, y_even):
    lo = pair_rows(field[:, 0:8, :][:, 0:4])
    hi = pair_rows(field[:, 56:64, :][:, 4:8])
    return jnp.where(y_even, hi, lo), jnp.where(y_even, lo, hi)


def prepare_kernel(route, slot, cond, code, c_a, c_b, m_own):
    g = lax.axis_index("gz")
    d = lax.axis_index("xy")
    rows = pl.ds(pl.multiple_of(g * 8, 8), 8)
    lane = lax.broadcasted_iota(jnp.int32, (8, 128), 1) % 32
    mine = (route[rows, :] == d).astype(jnp.int32)
    upto = mine
    for step in (1, 2, 4, 8, 16):
        upto = upto + jnp.where(lane >= step, pltpu.roll(upto, step, 1), 0)
    rank = upto - mine
    word = jnp.where(mine > 0, (slot[rows, :] + 1) << (5 * rank), 0)
    for step in (1, 2, 4, 8, 16):
        word = word + jnp.where(lane >= step, pltpu.roll(word, step, 1), 0)
    code[...] = word
    z_hi, z_lo = edge_starts(g)
    c_a[...] = cond[pl.ds(z_hi, 4)]
    c_b[...] = cond[pl.ds(z_lo, 4)]
    m_own[0], m_own[1] = edge_pairs(cond, d % 2 == 0)


def prepare(route, slot, cond):
    return pl.pallas_call(
        prepare_kernel,
        out_shape=(
            sds((8, 128), jnp.int32),
            sds((4, 64, 128), F32),
            sds((4, 64, 128), F32),
            sds((2, 8, 8, 128), F32),
        ),
        in_specs=[vspec()] * 3,
        out_specs=(vspec(),) * 4,
        compiler_params=params(),
        name="prepare",
    )(route, slot, cond)


def lists_kernel(code, count, entries):
    for j in range(16):
        count[j] = 0

    def source(s, carry):
        word = code[s // 4, (s % 4) * 32 + 31]
        for k in range(CAP):
            j = ((word >> (5 * k)) & 31) - 1

            @pl.when(j >= 0)
            def _():
                n = count[j]
                entries[j * 128 + n] = s * CAP + k
                count[j] = n + 1

        return carry

    lax.fori_loop(0, 32, source, 0)


def lists(code):
    return pl.pallas_call(
        lists_kernel,
        out_shape=(sds((16,), jnp.int32), sds((16 * 128,), jnp.int32)),
        in_specs=[sspec()],
        out_specs=(sspec(), sspec()),
        compiler_params=params(),
        name="lists",
    )(code)


def combine_kernel(recv, count, entries, v, z_a, z_b, y_c, y_d):
    g = lax.axis_index("gz")
    d = lax.axis_index("xy")
    for j in range(16):

        def record(i, acc):
            return acc + recv[entries[j * 128 + i]].astype(F32)

        block = lax.fori_loop(0, count[j], record, jnp.zeros((64, 128), F32))
        z0, y0 = (j // 8) * 8, (j % 8) * 8
        v[z0 : z0 + 8, y0 : y0 + 8, :] = block.reshape(8, 8, 128)
    z_hi, z_lo = edge_starts(g)
    z_a[...] = v[pl.ds(z_hi, 4)]
    z_b[...] = v[pl.ds(z_lo, 4)]
    y_c[...], y_d[...] = edge_pairs(v, d % 2 == 0)


def combine(recv, count, entries):
    return pl.pallas_call(
        combine_kernel,
        out_shape=(
            sds((16, 64, 128), F32),
            sds((4, 64, 128), F32),
            sds((4, 64, 128), F32),
            sds((8, 8, 128), F32),
            sds((8, 8, 128), F32),
        ),
        in_specs=[vspec(), sspec(), sspec()],
        out_specs=(vspec(),) * 5,
        compiler_params=params(),
        name="combine",
    )(recv, count, entries)


def strips_kernel(y_own, r_a, r_b, y_c, y_d):
    d = lax.axis_index("xy")
    y_even = d % 2 == 0
    y_c[0:8] = y_own[0]
    y_d[0:8] = y_own[1]
    for at, field in ((8, r_a), (10, r_b)):
        y_c[at : at + 2], y_d[at : at + 2] = edge_pairs(field, y_even)


def strips(y_own, r_a, r_b):
    return pl.pallas_call(
        strips_kernel,
        out_shape=(sds((12, 8, 128), F32),) * 2,
        in_specs=[vspec()] * 3,
        out_specs=(vspec(),) * 2,
        compiler_params=params(),
        name="strips",
    )(y_own, r_a, r_b)


def corners_kernel(r_a, r_b, k_c, k_d):
    d = lax.axis_index("xy")
    y_even = d % 2 == 0
    for at, field in ((0, r_a), (2, r_b)):
        k_c[at : at + 2], k_d[at : at + 2] = edge_pairs(field, y_even)


def corners(r_a, r_b):
    return pl.pallas_call(
        corners_kernel,
        out_shape=(sds((4, 8, 128), F32),) * 2,
        in_specs=[vspec()] * 2,
        out_specs=(vspec(),) * 2,
        compiler_params=params(),
        name="corners",
    )(r_a, r_b)


def split3(x):
    hi = x.astype(BF16)
    rest = x - hi.astype(F32)
    mid = rest.astype(BF16)
    lo = (rest - mid.astype(F32)).astype(BF16)
    return hi, mid, lo


def band(taps):
    i = lax.broadcasted_iota(jnp.int32, (128, 128), 0)
    j = lax.broadcasted_iota(jnp.int32, (128, 128), 1)
    m = jnp.zeros((128, 128), F32)
    for place, tap in enumerate(taps):
        if tap:
            m = jnp.where(i - j == place - 2, F32(tap), m)
    return m.astype(BF16)


S_TAPS = (1.0, 4.0, 6.0, 4.0, 1.0)
D_TAPS = (1.0, -8.0, 0.0, 8.0, -1.0)
NORM = 1.0 / (16.0 * 16.0 * 12.0)


def smooth5(a):
    return (a[0] + a[4]) + 4.0 * (a[1] + a[3]) + 6.0 * a[2]


def deriv5(a):
    return (a[0] - a[4]) + 8.0 * (a[3] - a[1])


def dot(a, b):
    return jnp.dot(a, b, preferred_element_type=F32)


def fill(ext, field, r_a, r_b, q_c, q_d, k_c=None, k_d=None):
    g = lax.axis_index("gz")
    d = lax.axis_index("xy")
    even = g % 2 == 0
    y_even = d % 2 == 0
    at_a = jnp.where(even, 20, 0)
    at_b = 20 - at_a
    low_in = (g > 0).astype(F32)
    high_in = (g < 7).astype(F32)
    keep_a = jnp.where(even, high_in, low_in)
    keep_b = jnp.where(even, low_in, high_in)
    left_in = (d > 0).astype(F32)
    right_in = (d < 31).astype(F32)
    zeros4 = jnp.zeros((4, 128), F32)
    ext[4:20, 8:72, :] = field[...]
    ext[pl.ds(at_a, 4), 8:72, :] = r_a[...] * keep_a
    ext[pl.ds(at_b, 4), 8:72, :] = r_b[...] * keep_b
    for z in range(24):
        if k_c is None or z < 16:
            c, e = q_c[z // 2], q_d[z // 2]
        else:
            c, e = k_c[z // 2 - 8], k_d[z // 2 - 8]
        lo = jnp.where(y_even, e, c)[4 * (z % 2) : 4 * (z % 2) + 4] * left_in
        hi = jnp.where(y_even, c, e)[4 * (z % 2) : 4 * (z % 2) + 4] * right_in
        if z < 16:
            place, keep = z + 4, 1.0
        elif z < 20:
            place, keep = at_a + (z - 16), keep_a
        else:
            place, keep = at_b + (z - 20), keep_b
        ext[place, 0:8, :] = jnp.concatenate([zeros4, lo * keep], axis=0)
        ext[place, 72:80, :] = jnp.concatenate([hi * keep, zeros4], axis=0)


def mix_xy(ext, sx, dx):
    weights = jnp.concatenate([band(S_TAPS), band(D_TAPS)], axis=1)
    twice = jnp.concatenate([weights, weights], axis=0)

    def along_x(i, carry):
        part = pl.ds(i * 6, 6)
        h, m, l = split3(ext[part].reshape(6 * 80, 128))
        both = dot(jnp.concatenate([h, m], axis=1), twice) + dot(l, weights)
        sx[part] = both[:, 0:128].reshape(6, 80, 128)
        dx[part] = both[:, 128:256].reshape(6, 80, 128)
        return carry

    lax.fori_loop(0, 4, along_x, 0, unroll=4)

    def along_y(z, carry):
        ss = [sx[z, 2 + i : 74 + i, :] for i in range(5)]
        tt = [dx[z, 2 + i : 74 + i, :] for i in range(5)]
        yx, xy, yy = smooth5(tt), deriv5(ss), smooth5(ss)
        dx[z, 4:76, :] = yx
        sx[z, 4:76, :] = xy
        ext[z, 4:76, :] = yy
        return carry

    lax.fori_loop(0, 24, along_y, 0, unroll=4)


def grad_tile(ext, sx, dx, z, tile):
    gx = smooth5([dx[z + i, tile, :] for i in range(5)])
    gy = smooth5([sx[z + i, tile, :] for i in range(5)])
    gz = deriv5([ext[z + i, tile, :] for i in range(5)])
    return gx, gy, gz


def model_kernel(cond, r_a, r_b, q_c, q_d, gm, ext, sx, dx):
    fill(ext, cond, r_a, r_b, q_c, q_d)
    mix_xy(ext, sx, dx)

    def tiles(t, carry):
        tile = pl.ds(pl.multiple_of(t * 8, 8), 8)
        for z in range(20):
            gx, gy, gz = grad_tile(ext, sx, dx, z, tile)
            gm[0, z, tile, :] = gx
            gm[1, z, tile, :] = gy
            gm[2, z, tile, :] = gz
        return carry

    lax.fori_loop(0, 10, tiles, 0)


def model(cond, r_a, r_b, q_c, q_d):
    return pl.pallas_call(
        model_kernel,
        out_shape=sds((3, 20, 80, 128), F32),
        in_specs=[vspec()] * 5,
        out_specs=vspec(),
        scratch_shapes=[pltpu.VMEM((24, 80, 128), F32)] * 3,
        compiler_params=params(),
        cost_estimate=pl.CostEstimate(flops=200_000_000, bytes_accessed=8_000_000, transcendentals=0),
        name="model",
    )(cond, r_a, r_b, q_c, q_d)


def stencil_kernel(v, r_a, r_b, q_c, q_d, k_c, k_d, gm, out, total, ext, sx, dx, back):
    g = lax.axis_index("gz")
    d = lax.axis_index("xy")
    low_in = (g > 0).astype(F32)
    high_in = (g < 7).astype(F32)
    fill(ext, v, r_a, r_b, q_c, q_d, k_c, k_d)
    mix_xy(ext, sx, dx)
    row = lax.broadcasted_iota(jnp.int32, (8, 128), 0)

    def cross(t, carry):
        y0 = pl.multiple_of(t * 8, 8)
        y = row + (y0 - 8)
        inside = jnp.where((y >= 0) | (d > 0), NORM, 0.0)
        inside = jnp.where((y < 64) | (d < 31), inside, 0.0)
        tile = pl.ds(y0, 8)
        adj = []
        for z in range(20):
            scale = inside
            if z < 2:
                scale = inside * low_in
            if z >= 18:
                scale = inside * high_in
            mx, my, mz = [gm[i, z, tile, :] * scale for i in range(3)]
            vx, vy, vz = [a * scale for a in grad_tile(ext, sx, dx, z, tile)]
            cx = my * vz - mz * vy
            cy = mz * vx - mx * vz
            cz = mx * vy - my * vx
            adj.append((vy * cz - vz * cy, vz * cx - vx * cz, vx * cy - vy * cx))
            if z >= 4:
                ax, ay, az = zip(*adj[z - 4 :])
                back[0, z - 4, tile, :] = smooth5(ax)
                back[1, z - 4, tile, :] = smooth5(ay)
                back[2, z - 4, tile, :] = deriv5(az)
        return carry

    lax.fori_loop(0, 10, cross, 0)

    w_s = band(S_TAPS)
    w_d = band(D_TAPS)
    w = jnp.concatenate([w_d, w_s], axis=0)

    w = jnp.concatenate([w, w, w], axis=0)

    p, q, r = [[back[j, :, 6 + k : 70 + k, :] for k in range(5)] for j in range(3)]
    us = split3(smooth5(p).reshape(1024, 128))
    ts = split3((deriv5(q) + smooth5(r)).reshape(1024, 128))
    both = [x for pair in zip(us, ts) for x in pair]
    acc = dot(jnp.concatenate(both, axis=1), w) * NORM
    out[...] = acc.reshape(16, 64, 128).astype(BF16)
    squares = jnp.sum((acc * acc).reshape(128, 8, 128), axis=0)
    total[...] = jnp.broadcast_to(jnp.sum(squares, axis=0, keepdims=True), (256, 128))


def stencil(v, r_a, r_b, q_c, q_d, k_c, k_d, gm):
    return pl.pallas_call(
        stencil_kernel,
        out_shape=(sds((16, 64, 128), BF16), sds((256, 128), F32)),
        in_specs=[vspec()] * 8,
        out_specs=(vspec(),) * 2,
        scratch_shapes=[
            pltpu.VMEM((24, 80, 128), F32),
            pltpu.VMEM((24, 80, 128), F32),
            pltpu.VMEM((24, 80, 128), F32),
            pltpu.VMEM((3, 16, 80, 128), F32),
        ],
        compiler_params=params(),
        name="stencil",
    )(v, r_a, r_b, q_c, q_d, k_c, k_d, gm)


def scale_kernel(cells, sums, *refs):
    pieces, out, held, sems = refs[:-3], refs[-3], refs[-2], refs[-1]
    g = lax.axis_index("gz")
    total = jnp.sum(sums[...], axis=0, keepdims=True)
    total = jnp.sum(total, axis=1, keepdims=True)
    scale = 1.0 / jnp.sqrt(total / cells + 1e-06)
    scale = jnp.broadcast_to(scale, (64, 128))
    left, right, across = lax.rem(g + 6, 8), lax.rem(g + 2, 8), lax.rem(g + 4, 8)
    owners = (g, left, right, across, g ^ 1, left ^ 1, right ^ 1, across ^ 1)
    copies = []
    for k, (piece, owner) in enumerate(zip(pieces, owners)):
        for z in range(16):
            held[k, z] = (piece[z].astype(F32) * scale).astype(BF16)
        copy = pltpu.make_async_copy(held.at[k], out.at[pl.ds(owner * 16, 16)], sems.at[k])
        copy.start()
        copies.append(copy)
    for copy in copies:
        copy.wait()


def scaled(cells, sums, pieces):
    return pl.pallas_call(
        functools.partial(scale_kernel, cells),
        out_shape=sds((128, 64, 128), BF16),
        in_specs=[vspec()] * (1 + len(pieces)),
        out_specs=pl.BlockSpec(memory_space=pl.ANY),
        scratch_shapes=[pltpu.VMEM((8, 16, 64, 128), BF16), pltpu.SemaphoreType.DMA((8,))],
        compiler_params=params(),
        name="scale",
    )(sums, *pieces)


def swap_odd(count):
    return [(i, (i + 1) % count if i % 2 else (i - 1) % count) for i in range(count)]


def swap_even(count):
    return [(i, i ^ 1) for i in range(count)]


def local(velocity, offset, interp_weight, route, dest_slot, conductivity):
    n_g = lax.axis_size("gz")
    n_x = lax.axis_size("xy")
    z_even, z_odd = swap_even(n_g), swap_odd(n_g)
    y_even, y_odd = swap_even(n_x), swap_odd(n_x)
    route = route.reshape(64, 128)
    send = pack(velocity, offset, interp_weight, route)
    send, route, dest_slot, conductivity = lax.optimization_barrier(
        (send, route, dest_slot, conductivity)
    )
    recv = lax.all_to_all(
        send.reshape(n_x, CAP * 64, 128), "xy", split_axis=0, concat_axis=0, tiled=True
    )
    code, c_a, c_b, m_own = prepare(route, dest_slot.reshape(64, 128), conductivity)
    rc_b = lax.ppermute(c_b, "gz", z_odd)
    rc_a = lax.ppermute(c_a, "gz", z_even)
    m_c, m_d = strips(m_own, rc_a, rc_b)
    qm_c = lax.ppermute(m_c, "xy", y_even)
    qm_d = lax.ppermute(m_d, "xy", y_odd)
    count, entries = lists(code)
    recv, count, entries, qm_c, qm_d = lax.optimization_barrier((recv, count, entries, qm_c, qm_d))
    v, z_a, z_b, y_c, y_d = combine(recv.reshape(n_x * CAP, 64, 128), count, entries)
    z_a, z_b, y_c, y_d, qm_c, qm_d = lax.optimization_barrier((z_a, z_b, y_c, y_d, qm_c, qm_d))
    r_b = lax.ppermute(z_b, "gz", z_odd)
    r_a = lax.ppermute(z_a, "gz", z_even)
    q_c = lax.ppermute(y_c, "xy", y_even)
    q_d = lax.ppermute(y_d, "xy", y_odd)
    gm = model(conductivity, rc_a, rc_b, qm_c, qm_d)
    k_c, k_d = corners(r_a, r_b)
    k_c = lax.ppermute(k_c, "xy", y_even)
    k_d = lax.ppermute(k_d, "xy", y_odd)
    grad, total = stencil(v, r_a, r_b, q_c, q_d, k_c, k_d, gm)
    core = swap_even(n_g)
    before = lax.ppermute(grad, "gz", [(i, (i + 2) % n_g) for i in range(n_g)])
    after = lax.ppermute(grad, "gz", [(i, (i - 2) % n_g) for i in range(n_g)])
    twin = lax.ppermute(grad, "gz", core)
    again, twin = lax.optimization_barrier((grad, twin))
    across = lax.ppermute(again, "gz", [(i, (i + 4) % n_g) for i in range(n_g)])
    sums = lax.all_to_all(total, ("gz", "xy"), 0, 0, tiled=True)
    before, after, across, sums = lax.optimization_barrier((before, after, across, sums))
    others = [lax.ppermute(piece, "gz", core) for piece in (before, after, across)]
    pieces = [grad, before, after, across, twin] + others
    cells = float(n_g * n_x * 16 * 64 * 128)
    return scaled(cells, sums, pieces)


def solution(mesh):
    in_specs = (
        P(("gz", "xy"), None, None, None),
        P(("gz", "xy")),
        P(("gz", "xy")),
        P(),
        P(),
        P("gz", "xy", None),
    )
    out_specs = P(None, "xy", None)
    return jax.shard_map(local, mesh=mesh, in_specs=in_specs, out_specs=out_specs, check_vma=False)
```

```python
import functools

import jax
import jax.numpy as jnp
from jax import lax
from jax.experimental import pallas as pl
from jax.experimental.pallas import tpu as pltpu
from jax.sharding import PartitionSpec as P

F32 = jnp.float32
BF16 = jnp.bfloat16
VMEM_LIMIT = 24 * 1024 * 1024
VMEM_ALL = 60 * 1024 * 1024
CAP = 4


def params(limit=VMEM_LIMIT):
    return pltpu.CompilerParams(vmem_limit_bytes=limit)


def vspec():
    return pl.BlockSpec(memory_space=pltpu.VMEM)


def sspec():
    return pl.BlockSpec(memory_space=pltpu.SMEM)


def sds(shape, dtype):
    return jax.ShapeDtypeStruct(shape, dtype)


def edge_starts(g):
    first = jnp.where(g % 2 == 0, 12, 0)
    return first, 12 - first


def pack_kernel(
    vel_any, off, wt, route_any, send, vel, out, route_s, count, sems
):
    g = lax.axis_index("gz")
    d = lax.axis_index("xy")
    rows = pl.ds(pl.multiple_of(g * 8, 8), 8)
    load = pltpu.make_async_copy(route_any.at[rows], route_s, sems.at[0])
    bricks = [
        pltpu.make_async_copy(vel_any.at[pl.ds(8 * i, 8)], vel.at[pl.ds(8 * i, 8)], sems.at[1 + i])
        for i in range(4)
    ]
    for copy in [load] + bricks:
        copy.start()
    for i in range(32):
        count[i] = 0
    load.wait()
    row = d // 4
    first = (d % 4) * 32
    x = lax.broadcasted_iota(jnp.int32, (64, 128), 1)
    for r in range(32):
        if r % 8 == 0:
            bricks[r // 8].wait()
        dest = route_s[row, first + r]
        k = count[dest]
        count[dest] = k + 1
        o = off[r]
        v = vel[r].reshape(64, 128)
        moved = jnp.where(x < 128 - o, pltpu.roll(v, (128 - o) % 128, 1), 0.0)
        out[r] = (moved * wt[r]).astype(BF16)
        pltpu.make_async_copy(out.at[r], send.at[dest * CAP + k], sems.at[5]).start()
    pltpu.make_async_copy(out, send.at[pl.ds(0, 32)], sems.at[5]).wait()


def pack(velocity, offset, weight, route):
    anywhere = pl.BlockSpec(memory_space=pl.ANY)
    return pl.pallas_call(
        pack_kernel,
        out_shape=sds((32 * CAP, 64, 128), BF16),
        in_specs=[anywhere, sspec(), sspec(), anywhere],
        out_specs=anywhere,
        scratch_shapes=[
            pltpu.VMEM((32, 8, 8, 128), F32),
            pltpu.VMEM((32, 64, 128), BF16),
            pltpu.SMEM((8, 128), jnp.int32),
            pltpu.SMEM((32,), jnp.int32),
            pltpu.SemaphoreType.DMA((6,)),
        ],
        compiler_params=params(VMEM_ALL),
        name="pack",
    )(velocity, offset, weight, route)


def pair_rows(block):
    n = block.shape[0] // 2
    return jnp.stack(
        [jnp.concatenate([block[2 * i], block[2 * i + 1]], axis=0) for i in range(n)]
    )


def edge_pairs(field, y_even):
    lo = pair_rows(field[:, 0:8, :][:, 0:4])
    hi = pair_rows(field[:, 56:64, :][:, 4:8])
    return jnp.where(y_even, hi, lo), jnp.where(y_even, lo, hi)


def prepare_kernel(route, slot, cond, code, c_a, c_b, m_own):
    g = lax.axis_index("gz")
    d = lax.axis_index("xy")
    rows = pl.ds(pl.multiple_of(g * 8, 8), 8)
    lane = lax.broadcasted_iota(jnp.int32, (8, 128), 1) % 32
    mine = (route[rows, :] == d).astype(jnp.int32)
    upto = mine
    for step in (1, 2, 4, 8, 16):
        upto = upto + jnp.where(lane >= step, pltpu.roll(upto, step, 1), 0)
    rank = upto - mine
    word = jnp.where(mine > 0, (slot[rows, :] + 1) << (5 * rank), 0)
    for step in (1, 2, 4, 8, 16):
        word = word + jnp.where(lane >= step, pltpu.roll(word, step, 1), 0)
    code[...] = word
    z_hi, z_lo = edge_starts(g)
    c_a[...] = cond[pl.ds(z_hi, 4)]
    c_b[...] = cond[pl.ds(z_lo, 4)]
    m_own[0], m_own[1] = edge_pairs(cond, d % 2 == 0)


def prepare(route, slot, cond):
    return pl.pallas_call(
        prepare_kernel,
        out_shape=(
            sds((8, 128), jnp.int32),
            sds((4, 64, 128), F32),
            sds((4, 64, 128), F32),
            sds((2, 8, 8, 128), F32),
        ),
        in_specs=[vspec()] * 3,
        out_specs=(vspec(),) * 4,
        compiler_params=params(),
        name="prepare",
    )(route, slot, cond)


def lists_kernel(code, count, entries):
    for j in range(16):
        count[j] = 0

    def source(s, carry):
        word = code[s // 4, (s % 4) * 32 + 31]
        for k in range(CAP):
            j = ((word >> (5 * k)) & 31) - 1

            @pl.when(j >= 0)
            def _():
                n = count[j]
                entries[j * 128 + n] = s * CAP + k
                count[j] = n + 1

        return carry

    lax.fori_loop(0, 32, source, 0)


def lists(code):
    return pl.pallas_call(
        lists_kernel,
        out_shape=(sds((16,), jnp.int32), sds((16 * 128,), jnp.int32)),
        in_specs=[sspec()],
        out_specs=(sspec(), sspec()),
        compiler_params=params(),
        name="lists",
    )(code)


def combine_kernel(recv, count, entries, v, z_a, z_b, y_c, y_d):
    g = lax.axis_index("gz")
    d = lax.axis_index("xy")
    for j in range(16):

        def record(i, acc):
            return acc + recv[entries[j * 128 + i]].astype(F32)

        block = lax.fori_loop(0, count[j], record, jnp.zeros((64, 128), F32))
        z0, y0 = (j // 8) * 8, (j % 8) * 8
        v[z0 : z0 + 8, y0 : y0 + 8, :] = block.reshape(8, 8, 128)
    z_hi, z_lo = edge_starts(g)
    z_a[...] = v[pl.ds(z_hi, 4)]
    z_b[...] = v[pl.ds(z_lo, 4)]
    y_c[...], y_d[...] = edge_pairs(v, d % 2 == 0)


def combine(recv, count, entries):
    return pl.pallas_call(
        combine_kernel,
        out_shape=(
            sds((16, 64, 128), F32),
            sds((4, 64, 128), F32),
            sds((4, 64, 128), F32),
            sds((8, 8, 128), F32),
            sds((8, 8, 128), F32),
        ),
        in_specs=[vspec(), sspec(), sspec()],
        out_specs=(vspec(),) * 5,
        compiler_params=params(),
        name="combine",
    )(recv, count, entries)


def strips_kernel(y_own, r_a, r_b, y_c, y_d):
    d = lax.axis_index("xy")
    y_even = d % 2 == 0
    y_c[0:8] = y_own[0]
    y_d[0:8] = y_own[1]
    for at, field in ((8, r_a), (10, r_b)):
        y_c[at : at + 2], y_d[at : at + 2] = edge_pairs(field, y_even)


def strips(y_own, r_a, r_b):
    return pl.pallas_call(
        strips_kernel,
        out_shape=(sds((12, 8, 128), F32),) * 2,
        in_specs=[vspec()] * 3,
        out_specs=(vspec(),) * 2,
        compiler_params=params(),
        name="strips",
    )(y_own, r_a, r_b)


def corners_kernel(r_a, r_b, k_c, k_d):
    d = lax.axis_index("xy")
    y_even = d % 2 == 0
    for at, field in ((0, r_a), (2, r_b)):
        k_c[at : at + 2], k_d[at : at + 2] = edge_pairs(field, y_even)


def corners(r_a, r_b):
    return pl.pallas_call(
        corners_kernel,
        out_shape=(sds((4, 8, 128), F32),) * 2,
        in_specs=[vspec()] * 2,
        out_specs=(vspec(),) * 2,
        compiler_params=params(),
        name="corners",
    )(r_a, r_b)


def split3(x):
    hi = x.astype(BF16)
    rest = x - hi.astype(F32)
    mid = rest.astype(BF16)
    lo = (rest - mid.astype(F32)).astype(BF16)
    return hi, mid, lo


def band(taps):
    i = lax.broadcasted_iota(jnp.int32, (128, 128), 0)
    j = lax.broadcasted_iota(jnp.int32, (128, 128), 1)
    m = jnp.zeros((128, 128), F32)
    for place, tap in enumerate(taps):
        if tap:
            m = jnp.where(i - j == place - 2, F32(tap), m)
    return m.astype(BF16)


S_TAPS = (1.0, 4.0, 6.0, 4.0, 1.0)
D_TAPS = (1.0, -8.0, 0.0, 8.0, -1.0)
NORM = 1.0 / (16.0 * 16.0 * 12.0)


def smooth5(a):
    return (a[0] + a[4]) + 4.0 * (a[1] + a[3]) + 6.0 * a[2]


def deriv5(a):
    return (a[0] - a[4]) + 8.0 * (a[3] - a[1])


def dot(a, b):
    return jnp.dot(a, b, preferred_element_type=F32)


def fill(ext, field, r_a, r_b, q_c, q_d, k_c=None, k_d=None):
    g = lax.axis_index("gz")
    d = lax.axis_index("xy")
    even = g % 2 == 0
    y_even = d % 2 == 0
    at_a = jnp.where(even, 20, 0)
    at_b = 20 - at_a
    low_in = (g > 0).astype(F32)
    high_in = (g < 7).astype(F32)
    keep_a = jnp.where(even, high_in, low_in)
    keep_b = jnp.where(even, low_in, high_in)
    left_in = (d > 0).astype(F32)
    right_in = (d < 31).astype(F32)
    zeros4 = jnp.zeros((4, 128), F32)
    ext[4:20, 8:72, :] = field[...]
    ext[pl.ds(at_a, 4), 8:72, :] = r_a[...] * keep_a
    ext[pl.ds(at_b, 4), 8:72, :] = r_b[...] * keep_b
    for z in range(24):
        if k_c is None or z < 16:
            c, e = q_c[z // 2], q_d[z // 2]
        else:
            c, e = k_c[z // 2 - 8], k_d[z // 2 - 8]
        lo = jnp.where(y_even, e, c)[4 * (z % 2) : 4 * (z % 2) + 4] * left_in
        hi = jnp.where(y_even, c, e)[4 * (z % 2) : 4 * (z % 2) + 4] * right_in
        if z < 16:
            place, keep = z + 4, 1.0
        elif z < 20:
            place, keep = at_a + (z - 16), keep_a
        else:
            place, keep = at_b + (z - 20), keep_b
        ext[place, 0:8, :] = jnp.concatenate([zeros4, lo * keep], axis=0)
        ext[place, 72:80, :] = jnp.concatenate([hi * keep, zeros4], axis=0)


def mix_xy(ext, sx, dx):
    weights = jnp.concatenate([band(S_TAPS), band(D_TAPS)], axis=1)
    twice = jnp.concatenate([weights, weights], axis=0)

    def along_x(i, carry):
        part = pl.ds(i * 6, 6)
        h, m, l = split3(ext[part].reshape(6 * 80, 128))
        both = dot(jnp.concatenate([h, m], axis=1), twice) + dot(l, weights)
        sx[part] = both[:, 0:128].reshape(6, 80, 128)
        dx[part] = both[:, 128:256].reshape(6, 80, 128)
        return carry

    lax.fori_loop(0, 4, along_x, 0, unroll=4)

    def along_y(z, carry):
        ss = [sx[z, 2 + i : 74 + i, :] for i in range(5)]
        tt = [dx[z, 2 + i : 74 + i, :] for i in range(5)]
        yx, xy, yy = smooth5(tt), deriv5(ss), smooth5(ss)
        dx[z, 4:76, :] = yx
        sx[z, 4:76, :] = xy
        ext[z, 4:76, :] = yy
        return carry

    lax.fori_loop(0, 24, along_y, 0, unroll=4)


def grad_tile(ext, sx, dx, z, tile):
    gx = smooth5([dx[z + i, tile, :] for i in range(5)])
    gy = smooth5([sx[z + i, tile, :] for i in range(5)])
    gz = deriv5([ext[z + i, tile, :] for i in range(5)])
    return gx, gy, gz


def model_kernel(cond, r_a, r_b, q_c, q_d, gm, ext, sx, dx):
    fill(ext, cond, r_a, r_b, q_c, q_d)
    mix_xy(ext, sx, dx)

    def tiles(t, carry):
        tile = pl.ds(pl.multiple_of(t * 8, 8), 8)
        for z in range(20):
            gx, gy, gz = grad_tile(ext, sx, dx, z, tile)
            gm[0, z, tile, :] = gx
            gm[1, z, tile, :] = gy
            gm[2, z, tile, :] = gz
        return carry

    lax.fori_loop(0, 10, tiles, 0)


def model(cond, r_a, r_b, q_c, q_d):
    return pl.pallas_call(
        model_kernel,
        out_shape=sds((3, 20, 80, 128), F32),
        in_specs=[vspec()] * 5,
        out_specs=vspec(),
        scratch_shapes=[pltpu.VMEM((24, 80, 128), F32)] * 3,
        compiler_params=params(),
        cost_estimate=pl.CostEstimate(flops=200_000_000, bytes_accessed=8_000_000, transcendentals=0),
        name="model",
    )(cond, r_a, r_b, q_c, q_d)


def stencil_kernel(v, r_a, r_b, q_c, q_d, k_c, k_d, gm, out, total, ext, sx, dx, back):
    g = lax.axis_index("gz")
    d = lax.axis_index("xy")
    low_in = (g > 0).astype(F32)
    high_in = (g < 7).astype(F32)
    fill(ext, v, r_a, r_b, q_c, q_d, k_c, k_d)
    mix_xy(ext, sx, dx)
    row = lax.broadcasted_iota(jnp.int32, (8, 128), 0)

    def cross(t, carry):
        y0 = pl.multiple_of(t * 8, 8)
        y = row + (y0 - 8)
        inside = jnp.where((y >= 0) | (d > 0), NORM, 0.0)
        inside = jnp.where((y < 64) | (d < 31), inside, 0.0)
        tile = pl.ds(y0, 8)
        adj = []
        for z in range(20):
            scale = inside
            if z < 2:
                scale = inside * low_in
            if z >= 18:
                scale = inside * high_in
            mx, my, mz = [gm[i, z, tile, :] * scale for i in range(3)]
            vx, vy, vz = [a * scale for a in grad_tile(ext, sx, dx, z, tile)]
            cx = my * vz - mz * vy
            cy = mz * vx - mx * vz
            cz = mx * vy - my * vx
            adj.append((vy * cz - vz * cy, vz * cx - vx * cz, vx * cy - vy * cx))
            if z >= 4:
                ax, ay, az = zip(*adj[z - 4 :])
                back[0, z - 4, tile, :] = smooth5(ax)
                back[1, z - 4, tile, :] = smooth5(ay)
                back[2, z - 4, tile, :] = deriv5(az)
        return carry

    lax.fori_loop(0, 10, cross, 0)

    w_s = band(S_TAPS)
    w_d = band(D_TAPS)
    w = jnp.concatenate([w_d, w_s], axis=0)

    w = jnp.concatenate([w, w, w], axis=0)

    p, q, r = [[back[j, :, 6 + k : 70 + k, :] for k in range(5)] for j in range(3)]
    us = split3(smooth5(p).reshape(1024, 128))
    ts = split3((deriv5(q) + smooth5(r)).reshape(1024, 128))
    both = [x for pair in zip(us, ts) for x in pair]
    acc = dot(jnp.concatenate(both, axis=1), w) * NORM
    out[...] = acc.reshape(16, 64, 128).astype(BF16)
    squares = jnp.sum((acc * acc).reshape(128, 8, 128), axis=0)
    total[...] = jnp.broadcast_to(jnp.sum(squares, axis=0, keepdims=True), (256, 128))


def stencil(v, r_a, r_b, q_c, q_d, k_c, k_d, gm):
    return pl.pallas_call(
        stencil_kernel,
        out_shape=(sds((16, 64, 128), BF16), sds((256, 128), F32)),
        in_specs=[vspec()] * 8,
        out_specs=(vspec(),) * 2,
        scratch_shapes=[
            pltpu.VMEM((24, 80, 128), F32),
            pltpu.VMEM((24, 80, 128), F32),
            pltpu.VMEM((24, 80, 128), F32),
            pltpu.VMEM((3, 16, 80, 128), F32),
        ],
        compiler_params=params(),
        name="stencil",
    )(v, r_a, r_b, q_c, q_d, k_c, k_d, gm)


def scale_kernel(cells, later, sums, *refs):
    pieces, out, held, sems = refs[:-3], refs[-3], refs[-2], refs[-1]
    if later:
        pieces = pieces[1:]
    g = lax.axis_index("gz")
    total = jnp.sum(sums[...], axis=0, keepdims=True)
    total = jnp.sum(total, axis=1, keepdims=True)
    scale = 1.0 / jnp.sqrt(total / cells + 1e-06)
    scale = jnp.broadcast_to(scale, (64, 128))
    left, right, across = lax.rem(g + 6, 8), lax.rem(g + 2, 8), lax.rem(g + 4, 8)
    owners = (g, left, right, across, g ^ 1)
    if later:
        owners = (left ^ 1, right ^ 1, across ^ 1)
    copies = []
    for k, (piece, owner) in enumerate(zip(pieces, owners)):
        for z in range(16):
            held[k, z] = (piece[z].astype(F32) * scale).astype(BF16)
        copy = pltpu.make_async_copy(held.at[k], out.at[pl.ds(owner * 16, 16)], sems.at[k])
        copy.start()
        copies.append(copy)
    for copy in copies:
        copy.wait()


def scaled(cells, sums, pieces, begun=None):
    anywhere = pl.BlockSpec(memory_space=pl.ANY)
    later = begun is not None
    n = len(pieces)
    return pl.pallas_call(
        functools.partial(scale_kernel, cells, later),
        out_shape=sds((128, 64, 128), BF16),
        in_specs=[vspec()] + [anywhere] * later + [vspec()] * n,
        out_specs=anywhere,
        scratch_shapes=[pltpu.VMEM((n, 16, 64, 128), BF16), pltpu.SemaphoreType.DMA((n,))],
        input_output_aliases={1: 0} if later else {},
        compiler_params=params(),
        cost_estimate=pl.CostEstimate(flops=n * 262144, bytes_accessed=n * 524288, transcendentals=0),
        name="scale",
    )(sums, *([begun] if later else []), *pieces)


def swap_odd(count):
    return [(i, (i + 1) % count if i % 2 else (i - 1) % count) for i in range(count)]


def swap_even(count):
    return [(i, i ^ 1) for i in range(count)]


def local(velocity, offset, interp_weight, route, dest_slot, conductivity):
    n_g = lax.axis_size("gz")
    n_x = lax.axis_size("xy")
    z_even, z_odd = swap_even(n_g), swap_odd(n_g)
    y_even, y_odd = swap_even(n_x), swap_odd(n_x)
    route = route.reshape(64, 128)
    send = pack(velocity, offset, interp_weight, route)
    send, route, dest_slot, conductivity = lax.optimization_barrier(
        (send, route, dest_slot, conductivity)
    )
    recv = lax.all_to_all(
        send.reshape(n_x, CAP * 64, 128), "xy", split_axis=0, concat_axis=0, tiled=True
    )
    code, c_a, c_b, m_own = prepare(route, dest_slot.reshape(64, 128), conductivity)
    rc_b = lax.ppermute(c_b, "gz", z_odd)
    rc_a = lax.ppermute(c_a, "gz", z_even)
    m_c, m_d = strips(m_own, rc_a, rc_b)
    qm_c = lax.ppermute(m_c, "xy", y_even)
    qm_d = lax.ppermute(m_d, "xy", y_odd)
    count, entries = lists(code)
    recv, count, entries, qm_c, qm_d = lax.optimization_barrier((recv, count, entries, qm_c, qm_d))
    v, z_a, z_b, y_c, y_d = combine(recv.reshape(n_x * CAP, 64, 128), count, entries)
    z_a, z_b, y_c, y_d, qm_c, qm_d = lax.optimization_barrier((z_a, z_b, y_c, y_d, qm_c, qm_d))
    r_b = lax.ppermute(z_b, "gz", z_odd)
    r_a = lax.ppermute(z_a, "gz", z_even)
    q_c = lax.ppermute(y_c, "xy", y_even)
    q_d = lax.ppermute(y_d, "xy", y_odd)
    gm = model(conductivity, rc_a, rc_b, qm_c, qm_d)
    k_c, k_d = corners(r_a, r_b)
    k_c = lax.ppermute(k_c, "xy", y_even)
    k_d = lax.ppermute(k_d, "xy", y_odd)
    grad, total = stencil(v, r_a, r_b, q_c, q_d, k_c, k_d, gm)
    core = swap_even(n_g)
    before = lax.ppermute(grad, "gz", [(i, (i + 2) % n_g) for i in range(n_g)])
    after = lax.ppermute(grad, "gz", [(i, (i - 2) % n_g) for i in range(n_g)])
    twin = lax.ppermute(grad, "gz", core)
    again, twin = lax.optimization_barrier((grad, twin))
    across = lax.ppermute(again, "gz", [(i, (i + 4) % n_g) for i in range(n_g)])
    sums = lax.all_to_all(total, ("gz", "xy"), 0, 0, tiled=True)
    before, after, across, sums = lax.optimization_barrier((before, after, across, sums))
    others = [lax.ppermute(piece, "gz", core) for piece in (before, after, across)]
    cells = float(n_g * n_x * 16 * 64 * 128)
    begun = scaled(cells, sums, [grad, before, after, across, twin])
    return scaled(cells, sums, others, begun)


def solution(mesh):
    in_specs = (
        P(("gz", "xy"), None, None, None),
        P(("gz", "xy")),
        P(("gz", "xy")),
        P(),
        P(),
        P("gz", "xy", None),
    )
    out_specs = P(None, "xy", None)
    return jax.shard_map(local, mesh=mesh, in_specs=in_specs, out_specs=out_specs, check_vma=False)
```
